32 devices in a mesh: dp: 16 (over z, y, core), ctx: 2 (over x).
Axes of the slice: x: 2, y: 2, z: 4, core: 2. Of those that a mesh axis runs over, the one named last changes fastest.
Arguments:
- query_proj: bfloat16 [32, 128, 4096], P('dp', 'ctx'), may hold values from -5 to 5
- key_proj: bfloat16 [32, 128, 1024], P('dp', 'ctx'), may hold values from -5 to 5
- value_proj: bfloat16 [32, 128, 1024], P('dp', 'ctx'), may hold values from -6 to 6
- grad_attn: bfloat16 [32, 128, 4096], P('dp', 'ctx'), may hold values from -6 to 6
- doc_lengths: int32 [32, 8], replicated, may hold values from 1 to 32, 128 in all within a row
- mask_tiles: int32 [32, 2, 2], replicated, may hold values from 0 to 1, as said below
- pair_flags: int32 [16], replicated, may hold values from 0 to 1, as said below
Outputs:
- attn_out: bfloat16 [32, 128, 4096], P('dp', 'ctx')
- grad_query: bfloat16 [32, 128, 4096], P('dp', 'ctx')
- grad_key: bfloat16 [32, 128, 1024], P('dp', 'ctx')
- grad_value: bfloat16 [32, 128, 1024], P('dp', 'ctx')
The draws below stay inside these ranges and needn't reach their ends.
Inputs may be any that keep to these rules, and one draw needn't show every extreme that they name: `doc_lengths`: each row sums to 128. mask_tiles[n, t, t] = 1 for every sequence n and tile t. pair_flags[r] = pair_flags[r XOR (8)] for every r.
All inputs are finite; a program needn't handle non-finite values.
Results may differ from the reference program's by a relative error of at most 0.03.
Values may be sent and summed in bfloat16 or wider, within the bound.
No kernel may reach another device: no remote copies, remote signals or barrier semaphores. Data moves between devices by JAX's collectives and lax.ppermute only.
A program may use at most 128 MiB of HBM per device.

```python
import math
import jax
import jax.numpy as jnp
import numpy as np
from jax import lax

QUERY_HEADS = 32
KEY_VALUE_HEADS = 8
HEAD_SIZE = 128
TILE = 64
NDOC = 8
QF = 4096
KF = 1024
PACKED_LENGTH = 128
NT = 2
SEQUENCE_COUNT = 32


def draw_query_proj(key, part):
    base_offset = jnp.clip(jax.random.normal(jax.random.fold_in(key, 1), (SEQUENCE_COUNT, PACKED_LENGTH, QUERY_HEADS * HEAD_SIZE), jnp.float32), -4.0, 4.0)
    return base_offset.astype(jnp.bfloat16)


def draw_key_proj(key, part):
    base_offset = jnp.clip(jax.random.normal(jax.random.fold_in(key, 2), (SEQUENCE_COUNT, PACKED_LENGTH, KEY_VALUE_HEADS * HEAD_SIZE), jnp.float32), -4.0, 4.0)
    return base_offset.astype(jnp.bfloat16)


def draw_mask_tiles(key, part):
    opened = jax.random.randint(jax.random.fold_in(key, 3), (SEQUENCE_COUNT, NT, NT), 0, 2)
    diagonal = jnp.arange(NT)[:, None] == jnp.arange(NT)[None, :]
    return jnp.where(diagonal[None, :, :], 1, opened).astype(jnp.int32)


def draw_pair_flags(key, part):
    half = SEQUENCE_COUNT // 4
    flags = jax.random.randint(jax.random.fold_in(key, 4), (half,), 0, 2)
    chosen = jax.random.randint(jax.random.fold_in(key, 5), (), 0, half)
    flags = jnp.where(jnp.arange(half) == chosen, 1, flags)
    return jnp.concatenate([flags, flags]).astype(jnp.int32)


def block_levels(own_key, extent, pieces, least, top_value):
    def one(dim, blocks):
        draws = jax.random.uniform(jax.random.fold_in(jax.random.fold_in(own_key, 6), dim), (blocks,), jnp.float32, least / len(pieces), top_value / len(pieces))
        return jnp.repeat(jnp.exp(draws), extent[dim] // blocks).reshape((-1,) + (1,) * (len(extent) - dim - 1))

    gain = one(*pieces[0])
    for cut in pieces[1:]:
        gain = gain * one(*cut)
    return gain


def split_up(number_of, total, reach, skew):
    weights = [(1 << 20) // math.isqrt(standing ** skew) + 1 for standing in range(2, number_of + 1)]
    rest, holding = total - reach - (number_of - 1), [1] * (number_of - 1)
    while rest > 0:
        candidates = [i for i in range(number_of - 1) if holding[i] < reach]
        pool, budget = sum([weights[i] for i in candidates]), rest
        for i in candidates:
            extra = min(reach - holding[i], max(1, budget * weights[i] // pool), rest)
            holding[i] = holding[i] + extra
            rest = rest - extra
    return np.array([reach] + holding)


def uneven(rng, amount, total, bound, slope):
    if amount == 2:
        one = jax.random.randint(rng, (), max(1, total - bound), min(bound, total - 1) + 1)
        return jnp.stack([one, total - one])
    tallies = jnp.asarray(split_up(amount, total, bound, slope), jnp.int32)
    twos = (amount - 1) // 2
    giver, sink = tallies[1:1 + 2 * twos:2], tallies[2:2 + 2 * twos:2]
    slack = jnp.minimum(giver - 1, bound - sink)
    moved = jax.random.randint(jax.random.fold_in(rng, 1), (twos,), 0, 1 << 20) % (slack + 1)
    tallies = tallies.at[1:1 + 2 * twos:2].set(giver - moved).at[2:2 + 2 * twos:2].set(sink + moved)
    return tallies[jax.random.permutation(jax.random.fold_in(rng, 2), amount)]


def bell_draw(own_key, extent, scale, reach, shards=(), kind=jnp.bfloat16):
    factor_of = block_levels(own_key, extent, shards, -0.22, 0.18) if shards else 1.0
    entries = jax.random.normal(own_key, extent, jnp.float32) * scale * factor_of
    return jnp.minimum(jnp.maximum(entries, -reach), reach).astype(kind)


def setup_inputs(seed: int = 0) -> dict:
    key_list = jax.random.split(jax.random.key(seed), 8)
    query_proj = draw_query_proj(jax.random.fold_in(key_list[7], 71), 0)
    key_proj = draw_key_proj(jax.random.fold_in(key_list[7], 71), 0)
    value_proj = bell_draw(key_list[2], (SEQUENCE_COUNT, PACKED_LENGTH, KF), 1.0, 6.0, ((0, 16), (1, 2)))
    grad_attn = bell_draw(key_list[3], (SEQUENCE_COUNT, PACKED_LENGTH, QF), 1.0, 6.0, ((0, 16), (1, 2)))
    doc_lengths = jax.vmap(lambda own: uneven(own, NDOC, PACKED_LENGTH, PACKED_LENGTH // 4, 2))(jax.random.split(key_list[4], SEQUENCE_COUNT)).reshape((SEQUENCE_COUNT, NDOC)).astype(jnp.int32)
    mask_tiles = draw_mask_tiles(jax.random.fold_in(key_list[7], 71), 0)
    pair_flags = draw_pair_flags(jax.random.fold_in(key_list[7], 71), 0)
    return dict(query_proj=query_proj, key_proj=key_proj, value_proj=value_proj, grad_attn=grad_attn, doc_lengths=doc_lengths, mask_tiles=mask_tiles, pair_flags=pair_flags)


def sequence_pass(query_rows, sequence_keys, sequence_values, sequence_gradients, lengths, tile_table):
    length_total = query_rows.shape[0]
    group_ratio = QUERY_HEADS // KEY_VALUE_HEADS
    scale = HEAD_SIZE ** -0.5
    positions = jnp.arange(length_total, dtype=jnp.int32)
    ends = jnp.cumsum(lengths.astype(jnp.int32))[:-1].astype(jnp.int32)
    doc_ids = jnp.sum((positions[:, None] >= ends[None, :]).astype(jnp.int32), axis=1)
    tile_map = jnp.repeat(jnp.repeat(tile_table, TILE, axis=0), TILE, axis=1) == 1
    allowed = (positions[None, :] <= positions[:, None]) & ((doc_ids[None, :] == doc_ids[:, None]) | (doc_ids[None, :] == 0)) & tile_map
    heads_of_queries = query_rows.reshape(length_total, KEY_VALUE_HEADS, group_ratio, HEAD_SIZE).astype(jnp.float32)
    heads_of_keys = sequence_keys.reshape(length_total, KEY_VALUE_HEADS, HEAD_SIZE).astype(jnp.float32)
    heads_of_values = sequence_values.reshape(length_total, KEY_VALUE_HEADS, HEAD_SIZE).astype(jnp.float32)
    head_gradients = sequence_gradients.reshape(length_total, KEY_VALUE_HEADS, group_ratio, HEAD_SIZE).astype(jnp.float32)
    scores = jnp.einsum("igrd,jgd->grij", heads_of_queries, heads_of_keys) * scale
    scores = jnp.where(allowed, scores, -1e30)
    peak = jnp.max(scores, axis=-1, keepdims=True)
    expd = jnp.where(allowed, jnp.exp(scores - peak), 0.0)
    probs = expd / jnp.sum(expd, axis=-1, keepdims=True)
    probs_b = probs.astype(jnp.bfloat16).astype(jnp.float32)
    attn = jnp.einsum("grij,jgd->igrd", probs_b, heads_of_values).astype(jnp.bfloat16)
    delta = jnp.transpose(jnp.sum(head_gradients * attn.astype(jnp.float32), axis=-1), (1, 2, 0))
    value_gradient = jnp.einsum("grij,igrd->jgd", probs_b, head_gradients)
    dprobs = jnp.einsum("igrd,jgd->grij", head_gradients, heads_of_values)
    dscores = (probs * (dprobs - delta[..., None]) * scale).astype(jnp.bfloat16).astype(jnp.float32)
    grad_q = jnp.einsum("grij,jgd->igrd", dscores, heads_of_keys)
    key_gradient = jnp.einsum("grij,igrd->jgd", dscores, heads_of_queries)
    return (attn.reshape(length_total, QUERY_HEADS * HEAD_SIZE),
            grad_q.astype(jnp.bfloat16).reshape(length_total, QUERY_HEADS * HEAD_SIZE),
            key_gradient.astype(jnp.bfloat16).reshape(length_total, KEY_VALUE_HEADS * HEAD_SIZE),
            value_gradient.astype(jnp.bfloat16).reshape(length_total, KEY_VALUE_HEADS * HEAD_SIZE))


def reference(query_proj, key_proj, value_proj, grad_attn, doc_lengths, mask_tiles, pair_flags):
    ranks = SEQUENCE_COUNT // 2
    seq_index = jnp.arange(SEQUENCE_COUNT, dtype=jnp.int32)
    owner = (seq_index // 2).astype(jnp.int32)
    partner = jnp.bitwise_xor(owner, ranks // 2).astype(jnp.int32)
    flags = jnp.take(pair_flags, owner, axis=0)
    order = jnp.where((seq_index % 2 == 1) & (flags == 1), 2 * partner + 1, seq_index).astype(jnp.int32)

    def one_sequence(index):
        return sequence_pass(query_proj[index], key_proj[index], value_proj[index], grad_attn[index], doc_lengths[index], mask_tiles[index])

    attn_out, grad_query, grad_key, grad_value = lax.map(one_sequence, order)
    return (attn_out, grad_query, grad_key, grad_value)
```

```python
import functools

import jax
import jax.numpy as jnp
from jax import lax
from jax.experimental import pallas as pl
from jax.experimental.pallas import tpu as pltpu
from jax.sharding import PartitionSpec as P

QUERY_HEADS = 32
KEY_VALUE_HEADS = 8
HEAD_SIZE = 128
GROUP_RATIO = QUERY_HEADS // KEY_VALUE_HEADS
SCALE = HEAD_SIZE ** (-0.5)
GROUPS_PER_STEP = 2
NT_DIMS = (((1,), (1,)), ((), ()))
TN_DIMS = (((0,), (0,)), ((), ()))
NN_DIMS = (((1,), (0,)), ((), ()))


def dot(a, b, dims):
    return lax.dot_general(a, b, dims, preferred_element_type=jnp.float32)


def masks(lengths_ref, tiles_ref, seq, rows, lanes):
    ctx = lax.axis_index("ctx")
    key_index = lax.broadcasted_iota(jnp.int32, (2 * rows, lanes), 0)
    lane = lax.broadcasted_iota(jnp.int32, (2 * rows, lanes), 1)
    col_pos = key_index + (ctx - 1) * rows
    row_pos = lax.rem(lane, rows) + ctx * rows
    col_doc = jnp.zeros_like(col_pos)
    row_doc = jnp.zeros_like(row_pos)
    end = jnp.int32(0)
    for d in range(lengths_ref.shape[1] - 1):
        end = end + lengths_ref[seq, d]
        col_doc = col_doc + (col_pos >= end).astype(jnp.int32)
        row_doc = row_doc + (row_pos >= end).astype(jnp.int32)
    first_open = jnp.where(ctx > 0, tiles_ref[seq, ctx, jnp.maximum(ctx - 1, 0)], 0)
    seen = (key_index >= rows) | (first_open == 1)
    same = col_doc == row_doc
    query = (col_doc == 0) & (col_pos >= 0)
    own = same & (col_pos >= 0)
    allowed = (col_pos <= row_pos) & (own | query) & seen
    return allowed, own, query


def stacked_heads(block, rows):
    return jnp.concatenate(
        [block[:, h * HEAD_SIZE : (h + 1) * HEAD_SIZE] for h in range(GROUP_RATIO)], axis=0
    )


def spread_heads(value, rows):
    return jnp.concatenate([value[h * rows : (h + 1) * rows] for h in range(GROUP_RATIO)], axis=1)


def folded(value, bound):
    total = value[:bound]
    for b in range(1, value.shape[0] // bound):
        total = total + value[b * bound : (b + 1) * bound]
    return total


def attention_body(
    packed, slots, first_slot, rows, q_ref, g_ref, k_ref, v_ref, kv_ref, lengths_ref, tiles_ref, *rest
):
    if packed:
        pack_ref, own_ref, other_ref, bias_ref, same_ref = rest
    else:
        attn_ref, gq_ref, own_ref, other_ref, bias_ref = rest
    lanes = GROUP_RATIO * rows
    slot = first_slot + pl.program_id(0)

    @pl.when(pl.program_id(1) == 0)
    def _():
        seq = 2 * lax.axis_index("dp") + slot
        allowed, own, _ = masks(lengths_ref, tiles_ref, seq, rows, lanes)
        bias_ref[...] = jnp.where(allowed, 0.0, -1e30)
        if packed:
            same_ref[...] = jnp.where(own, 1.0, 0.0)

    for u in range(GROUPS_PER_STEP):
        feats = pl.ds(u * HEAD_SIZE, HEAD_SIZE)
        wide = pl.ds(u * GROUP_RATIO * HEAD_SIZE, GROUP_RATIO * HEAD_SIZE)
        q = stacked_heads(q_ref[:, wide], rows)
        g = stacked_heads(g_ref[:, wide], rows)
        k = jnp.concatenate([kv_ref[0, :, feats], k_ref[:, feats]], axis=0)
        v = jnp.concatenate([kv_ref[1, :, feats], v_ref[:, feats]], axis=0)
        scores = dot(k, q, NT_DIMS) * SCALE + bias_ref[...]
        peak = jnp.max(scores, axis=0, keepdims=True)
        expd = jnp.exp(scores - peak)
        probs = expd * (1.0 / jnp.sum(expd, axis=0, keepdims=True))
        dprobs = dot(v, g, NT_DIMS)
        delta = jnp.sum(probs * dprobs, axis=0, keepdims=True)
        dscores = probs * (dprobs - delta) * SCALE
        probs_b = probs.astype(jnp.bfloat16)
        dscores_b = dscores.astype(jnp.bfloat16)
        key_grad = dot(dscores_b, q, NN_DIMS)
        value_grad = dot(probs_b, g, NN_DIMS)
        own_ref[0, :, feats] = key_grad[rows:]
        own_ref[1, :, feats] = value_grad[rows:]
        other_ref[0, :, feats] = key_grad[:rows].astype(jnp.bfloat16)
        other_ref[1, :, feats] = value_grad[:rows].astype(jnp.bfloat16)
        if packed:
            bound = rows // 2
            same = same_ref[...] > 0.5
            span = pl.ds(u * lanes, lanes)
            for which, value in ((0, probs), (1, dscores)):
                near = folded(jnp.where(same, value, 0.0), bound)
                far = folded(jnp.where(same, 0.0, value), bound)
                pack_ref[which, :, span] = jnp.concatenate([near, far], axis=0).astype(jnp.bfloat16)
        else:
            attn_ref[:, wide] = spread_heads(dot(probs_b, v, TN_DIMS), rows).astype(jnp.bfloat16)
            gq_ref[:, wide] = spread_heads(dot(dscores_b, k, TN_DIMS), rows).astype(jnp.bfloat16)


def attention(packed, first_slot, slots, q, g, k, v, kv_first, lengths, tiles):
    rows = q.shape[1]
    lanes = GROUP_RATIO * rows
    wide = GROUPS_PER_STEP * GROUP_RATIO * HEAD_SIZE
    feats = GROUPS_PER_STEP * HEAD_SIZE
    of_q = pl.BlockSpec((None, rows, wide), lambda s, i: (s + first_slot, 0, i))
    of_k = pl.BlockSpec((None, rows, feats), lambda s, i: (s + first_slot, 0, i))
    of_kv = pl.BlockSpec((None, 2, rows, feats), lambda s, i: (s, 0, 0, i))
    smem = pl.BlockSpec(memory_space=pltpu.SMEM)
    partial = (slots, 2, rows, KEY_VALUE_HEADS * HEAD_SIZE)
    out_shape = [jax.ShapeDtypeStruct(partial, jnp.float32), jax.ShapeDtypeStruct(partial, jnp.bfloat16)]
    out_specs = [of_kv, of_kv]
    scratch = [pltpu.VMEM((2 * rows, lanes), jnp.float32)]
    if packed:
        out_shape.insert(0, jax.ShapeDtypeStruct((2, rows, KEY_VALUE_HEADS * lanes), jnp.bfloat16))
        out_specs.insert(0, pl.BlockSpec((2, rows, GROUPS_PER_STEP * lanes), lambda s, i: (0, 0, i)))
        scratch = scratch * 2
    else:
        out_shape = [jax.ShapeDtypeStruct(q.shape, q.dtype)] * 2 + out_shape
        out_specs = [of_q, of_q] + out_specs
    return pl.pallas_call(
        functools.partial(attention_body, packed, slots, first_slot, rows),
        grid=(slots, KEY_VALUE_HEADS // GROUPS_PER_STEP),
        in_specs=[of_q, of_q, of_k, of_k, of_kv, smem, smem],
        out_specs=out_specs,
        out_shape=out_shape,
        scratch_shapes=scratch,
        compiler_params=pltpu.CompilerParams(vmem_limit_bytes=32 * 2**20),
        cost_estimate=pl.CostEstimate(
            flops=slots * 12 * QUERY_HEADS * rows * 2 * rows * HEAD_SIZE,
            bytes_accessed=slots * 6 * rows * QUERY_HEADS * HEAD_SIZE * 2,
            transcendentals=slots * QUERY_HEADS * rows * 2 * rows,
        ),
    )(q, g, k, v, kv_first, lengths, tiles)


def rebuild_body(rows, pack_ref, near_ref, first_ref, lengths_ref, tiles_ref, _a, _b, attn_ref, gq_ref, own_ref, query_ref):
    lanes = GROUP_RATIO * rows
    bound = rows // 2

    @pl.when(pl.program_id(0) == 0)
    def _():
        partner = jnp.bitwise_xor(lax.axis_index("dp"), lax.axis_size("dp") // 2)
        _, own, query = masks(lengths_ref, tiles_ref, 2 * partner + 1, rows, lanes)
        own_ref[...] = jnp.where(own, 1.0, 0.0)
        query_ref[...] = jnp.where(query, 1.0, 0.0)

    for u in range(GROUPS_PER_STEP):
        feats = pl.ds(u * HEAD_SIZE, HEAD_SIZE)
        wide = pl.ds(u * GROUP_RATIO * HEAD_SIZE, GROUP_RATIO * HEAD_SIZE)
        span = pl.ds(u * lanes, lanes)
        for which, out_ref in ((1, attn_ref), (0, gq_ref)):
            side = jnp.concatenate([first_ref[which, :, feats], near_ref[which, :, feats]], axis=0)
            coded = pack_ref[1 - which, :, span].astype(jnp.float32)
            copies = 2 * rows // bound
            near = jnp.concatenate([coded[:bound]] * copies, axis=0)
            far = jnp.concatenate([coded[bound:]] * copies, axis=0)
            value = jnp.where(own_ref[...] > 0.5, near, jnp.where(query_ref[...] > 0.5, far, 0.0))
            out = dot(value.astype(jnp.bfloat16), side, TN_DIMS)
            out_ref[:, wide] = spread_heads(out, rows).astype(jnp.bfloat16)


def rebuild(pack, kv_near, kv_first, lengths, tiles, attn, gq):
    rows = attn.shape[1]
    lanes = GROUP_RATIO * rows
    wide = GROUPS_PER_STEP * GROUP_RATIO * HEAD_SIZE
    feats = GROUPS_PER_STEP * HEAD_SIZE
    of_kv = pl.BlockSpec((2, rows, feats), lambda i: (0, 0, i))
    of_q = pl.BlockSpec((None, rows, wide), lambda i: (1, 0, i))
    smem = pl.BlockSpec(memory_space=pltpu.SMEM)
    anywhere = pl.BlockSpec(memory_space=pl.ANY)
    return pl.pallas_call(
        functools.partial(rebuild_body, rows),
        grid=(KEY_VALUE_HEADS // GROUPS_PER_STEP,),
        in_specs=[
            pl.BlockSpec((2, rows, GROUPS_PER_STEP * lanes), lambda i: (0, 0, i)),
            of_kv,
            of_kv,
            smem,
            smem,
            anywhere,
            anywhere,
        ],
        out_specs=[of_q, of_q],
        out_shape=[jax.ShapeDtypeStruct(attn.shape, attn.dtype)] * 2,
        scratch_shapes=[pltpu.VMEM((2 * rows, lanes), jnp.float32)] * 2,
        input_output_aliases={5: 0, 6: 1},
        compiler_params=pltpu.CompilerParams(vmem_limit_bytes=32 * 2**20),
    )(pack, kv_near, kv_first, lengths, tiles, attn, gq)


def to_next(value):
    return lax.ppermute(value, "ctx", [(0, 1)])


def to_owner(value):
    return lax.ppermute(value, "ctx", [(1, 0)])


def to_partner(value):
    size = lax.axis_size("dp")
    return lax.ppermute(value, "dp", [(s, s ^ (size // 2)) for s in range(size)])


def joined(own, arrived):
    return (own + arrived.astype(jnp.float32)).astype(jnp.bfloat16)


def stay(q, k, v, g, lengths, tiles):
    kv_first = jnp.stack([to_next(k), to_next(v)], axis=1)
    attn, gq, own, other = attention(False, 0, 2, q, g, k, v, kv_first, lengths, tiles)
    grads = joined(own, to_owner(other))
    return attn, gq, grads[:, 0], grads[:, 1]


def trade(q, k, v, g, lengths, tiles):
    kv_second = jnp.stack([k[1], v[1]])
    first_second = to_next(kv_second)
    kv_partner = to_partner(kv_second)
    first_zero = to_next(jnp.stack([k[0], v[0]]))
    pack, own_second, other_second = attention(True, 1, 1, q, g, k, v, first_second[None], lengths, tiles)
    pack_partner = to_partner(pack)
    grads_second = joined(own_second[0], to_owner(other_second[0]))
    grads_partner = to_partner(grads_second)
    first_partner = to_next(kv_partner)
    attn, gq, own_zero, other_zero = attention(
        False, 0, 1, q, g, k, v, first_zero[None], lengths, tiles
    )
    grads_zero = joined(own_zero[0], to_owner(other_zero[0]))
    attn, gq = rebuild(pack_partner, kv_partner, first_partner, lengths, tiles, attn, gq)
    return (
        attn,
        gq,
        jnp.stack([grads_zero[0], grads_partner[0]]),
        jnp.stack([grads_zero[1], grads_partner[1]]),
    )


def two_rank_shards(query_proj, key_proj, value_proj, grad_attn, doc_lengths, mask_tiles, pair_flags):
    dp_rank = lax.axis_index("dp")
    flag = lax.dynamic_index_in_dim(pair_flags, dp_rank, 0, keepdims=False)
    return lax.cond(
        flag == 1,
        trade,
        stay,
        query_proj,
        key_proj,
        value_proj,
        grad_attn,
        doc_lengths,
        mask_tiles,
    )


def from_partner(value, axis, distance):
    mask = 2**distance
    pairs = [(source, source ^ mask) for source in range(lax.axis_size(axis))]
    return lax.ppermute(value, axis, pairs)


def sequence_core(
    query_rows, sequence_keys, sequence_values, sequence_gradients, lengths, tile_table, row_start
):
    rows = query_rows.shape[0]
    length_total = sequence_keys.shape[0]
    groups = sequence_keys.shape[1] // HEAD_SIZE
    group_ratio = QUERY_HEADS // KEY_VALUE_HEADS
    scale = HEAD_SIZE ** (-0.5)
    row_pos = row_start + jnp.arange(rows, dtype=jnp.int32)
    col_pos = jnp.arange(length_total, dtype=jnp.int32)
    ends = jnp.cumsum(lengths)[:-1]
    row_doc = jnp.sum((row_pos[:, None] >= ends[None, :]).astype(jnp.int32), axis=1)
    col_doc = jnp.sum((col_pos[:, None] >= ends[None, :]).astype(jnp.int32), axis=1)
    tile_count = tile_table.shape[0]
    tile_len = length_total // tile_count
    tile_ids = jnp.arange(tile_count, dtype=jnp.int32)
    row_pick = ((row_pos // tile_len)[:, None] == tile_ids[None, :]).astype(jnp.float32)
    col_pick = ((col_pos // tile_len)[:, None] == tile_ids[None, :]).astype(jnp.float32)
    tile_map = jnp.dot(jnp.dot(row_pick, tile_table.astype(jnp.float32)), col_pick.T) > 0.5
    allowed = (
        (col_pos[None, :] <= row_pos[:, None])
        & ((col_doc[None, :] == row_doc[:, None]) | (col_doc[None, :] == 0))
        & tile_map
    )
    heads_of_queries = query_rows.reshape(rows, groups, group_ratio, HEAD_SIZE)
    heads_of_keys = sequence_keys.reshape(length_total, groups, HEAD_SIZE)
    heads_of_values = sequence_values.reshape(length_total, groups, HEAD_SIZE)
    head_gradients = sequence_gradients.reshape(rows, groups, group_ratio, HEAD_SIZE)
    scores = (
        jnp.einsum(
            "igrd,jgd->grij", heads_of_queries, heads_of_keys, preferred_element_type=jnp.float32
        )
        * scale
    )
    scores = jnp.where(allowed, scores, -1e30)
    peak = jnp.max(scores, axis=-1, keepdims=True)
    expd = jnp.where(allowed, jnp.exp(scores - peak), 0.0)
    probs = expd / jnp.sum(expd, axis=-1, keepdims=True)
    probs_b = probs.astype(jnp.bfloat16)
    attn = jnp.einsum(
        "grij,jgd->igrd", probs_b, heads_of_values, preferred_element_type=jnp.float32
    ).astype(jnp.bfloat16)
    delta = jnp.transpose(
        jnp.sum(head_gradients.astype(jnp.float32) * attn.astype(jnp.float32), axis=-1), (1, 2, 0)
    )
    value_gradient = jnp.einsum(
        "grij,igrd->jgd", probs_b, head_gradients, preferred_element_type=jnp.float32
    )
    dprobs = jnp.einsum(
        "igrd,jgd->grij", head_gradients, heads_of_values, preferred_element_type=jnp.float32
    )
    dscores = (probs * (dprobs - delta[..., None]) * scale).astype(jnp.bfloat16)
    grad_q = jnp.einsum(
        "grij,jgd->igrd", dscores, heads_of_keys, preferred_element_type=jnp.float32
    )
    key_gradient = jnp.einsum(
        "grij,igrd->jgd", dscores, heads_of_queries, preferred_element_type=jnp.float32
    )
    return (
        attn.reshape(rows, -1),
        grad_q.astype(jnp.bfloat16).reshape(rows, -1),
        key_gradient.reshape(length_total, -1),
        value_gradient.reshape(length_total, -1),
    )


def attend(query_rows, keys_in, values_in, grads_in, lengths_all, tiles_all, first_id, second_id):
    seq_ids = jnp.stack([first_id, second_id])
    lengths_pair = jnp.take(lengths_all, seq_ids, axis=0)
    tiles_pair = jnp.take(tiles_all, seq_ids, axis=0)
    ctx_rank = lax.axis_index("ctx")
    seq_dev = query_rows.shape[1]
    keys_all, values_all = (
        lax.all_gather(keys_in, "ctx", axis=1, tiled=True),
        lax.all_gather(values_in, "ctx", axis=1, tiled=True),
    )
    pieces = [
        sequence_core(
            query_rows[seq_slot],
            keys_all[seq_slot],
            values_all[seq_slot],
            grads_in[seq_slot],
            lengths_pair[seq_slot],
            tiles_pair[seq_slot],
            ctx_rank * seq_dev,
        )
        for seq_slot in range(2)
    ]
    attn = jnp.stack([pieces[0][0], pieces[1][0]])
    grad_q = jnp.stack([pieces[0][1], pieces[1][1]])
    key_terms = jnp.stack([pieces[0][2], pieces[1][2]])
    value_terms = jnp.stack([pieces[0][3], pieces[1][3]])
    key_sums, value_sums = (
        lax.psum_scatter(key_terms, "ctx", scatter_dimension=1, tiled=True),
        lax.psum_scatter(value_terms, "ctx", scatter_dimension=1, tiled=True),
    )
    return (attn, grad_q, key_sums.astype(jnp.bfloat16), value_sums.astype(jnp.bfloat16))


def take_second(mine, arrived, swapped):
    return jnp.stack([mine[0], jnp.where(swapped, arrived, mine[1])])


def shards(query_proj, key_proj, value_proj, grad_attn, doc_lengths, mask_tiles, pair_flags):
    dp_size = lax.axis_size("dp")
    dp_rank = lax.axis_index("dp")
    far_bit = dp_size.bit_length() - 2
    partner = jnp.bitwise_xor(dp_rank, dp_size // 2)
    pair_flag = lax.dynamic_index_in_dim(pair_flags, dp_rank, 0, keepdims=False)
    swapped = pair_flag == 1
    first_id = 2 * dp_rank
    second_id = jnp.where(swapped, 2 * partner + 1, 2 * dp_rank + 1)
    arrived = from_partner((query_proj[1], key_proj[1], value_proj[1], grad_attn[1]), "dp", far_bit)
    query_now = take_second(query_proj, arrived[0], swapped)
    key_now = take_second(key_proj, arrived[1], swapped)
    value_now = take_second(value_proj, arrived[2], swapped)
    grad_now = take_second(grad_attn, arrived[3], swapped)
    return attend(
        query_now, key_now, value_now, grad_now, doc_lengths, mask_tiles, first_id, second_id
    )


def solution(mesh):
    in_specs = (
        P("dp", "ctx", None),
        P("dp", "ctx", None),
        P("dp", "ctx", None),
        P("dp", "ctx", None),
        P(),
        P(),
        P(),
    )
    out_specs = (
        P("dp", "ctx", None),
        P("dp", "ctx", None),
        P("dp", "ctx", None),
        P("dp", "ctx", None),
    )
    form = two_rank_shards if mesh.shape["ctx"] == 2 else shards
    return jax.shard_map(form, mesh=mesh, in_specs=in_specs, out_specs=out_specs, check_vma=False)
```

```python
import functools

import jax
import jax.numpy as jnp
from jax import lax
from jax.experimental import pallas as pl
from jax.experimental.pallas import tpu as pltpu
from jax.sharding import PartitionSpec as P

QUERY_HEADS = 32
KEY_VALUE_HEADS = 8
HEAD_SIZE = 128
GROUP_RATIO = QUERY_HEADS // KEY_VALUE_HEADS
SCALE = HEAD_SIZE ** (-0.5)
GROUPS_PER_STEP = 4
CHEAP = pl.CostEstimate(flops=1, bytes_accessed=1, transcendentals=0)
NT_DIMS = (((1,), (1,)), ((), ()))
TN_DIMS = (((0,), (0,)), ((), ()))
NN_DIMS = (((1,), (0,)), ((), ()))


def dot(a, b, dims):
    return lax.dot_general(a, b, dims, preferred_element_type=jnp.float32)


def masks(lengths_ref, tiles_ref, seq, rows, lanes):
    ctx = lax.axis_index("ctx")
    key_index = lax.broadcasted_iota(jnp.int32, (2 * rows, lanes), 0)
    lane = lax.broadcasted_iota(jnp.int32, (2 * rows, lanes), 1)
    col_pos = key_index + (ctx - 1) * rows
    row_pos = lax.rem(lane, rows) + ctx * rows
    col_doc = jnp.zeros_like(col_pos)
    row_doc = jnp.zeros_like(row_pos)
    end = jnp.int32(0)
    for d in range(lengths_ref.shape[0] - 1):
        end = end + lengths_ref[d, seq]
        col_doc = col_doc + (col_pos >= end).astype(jnp.int32)
        row_doc = row_doc + (row_pos >= end).astype(jnp.int32)
    first_open = jnp.where(ctx > 0, tiles_ref[ctx, jnp.maximum(ctx - 1, 0), seq], 0)
    seen = (key_index >= rows) | (first_open == 1)
    same = col_doc == row_doc
    query = (col_doc == 0) & (col_pos >= 0)
    own = same & (col_pos >= 0)
    allowed = (col_pos <= row_pos) & (own | query) & seen
    return allowed, own, query


def stacked_heads(block, rows):
    return jnp.concatenate(
        [block[:, h * HEAD_SIZE : (h + 1) * HEAD_SIZE] for h in range(GROUP_RATIO)], axis=0
    )


def spread_heads(value, rows):
    return jnp.concatenate([value[h * rows : (h + 1) * rows] for h in range(GROUP_RATIO)], axis=1)


def folded(value, bound):
    total = value[:bound]
    for b in range(1, value.shape[0] // bound):
        total = total + value[b * bound : (b + 1) * bound]
    return total


def attention_body(
    packed, first_slot, rows, q_ref, g_ref, k_ref, v_ref, kf_ref, vf_ref, lengths_ref, tiles_ref, *rest
):
    passed, rest = rest[:-5], rest[-5:]
    if packed:
        pack_ref, own_ref, other_ref, bias_ref, same_ref = rest
    else:
        attn_ref, gq_ref, own_ref, other_ref, bias_ref = rest
    lanes = GROUP_RATIO * rows
    slot = first_slot + pl.program_id(0)

    @pl.when(pl.program_id(1) == 0)
    def _():
        seq = 2 * lax.axis_index("dp") + slot
        allowed, own, _ = masks(lengths_ref, tiles_ref, seq, rows, lanes)
        bias_ref[...] = jnp.where(allowed, 0.0, -1e30)
        if packed:
            same_ref[...] = jnp.where(own, 1.0, 0.0)

    for u in range(GROUPS_PER_STEP):
        feats = pl.ds(u * HEAD_SIZE, HEAD_SIZE)
        wide = pl.ds(u * GROUP_RATIO * HEAD_SIZE, GROUP_RATIO * HEAD_SIZE)
        q = stacked_heads(q_ref[:, wide], rows)
        g = stacked_heads(g_ref[:, wide], rows)
        k = jnp.concatenate([kf_ref[:, feats], k_ref[:, feats]], axis=0)
        v = jnp.concatenate([vf_ref[:, feats], v_ref[:, feats]], axis=0)
        scores = dot(k, q, NT_DIMS) * SCALE + bias_ref[...]
        peak = jnp.max(scores, axis=0, keepdims=True)
        expd = jnp.exp(scores - peak)
        probs = expd * (1.0 / jnp.sum(expd, axis=0, keepdims=True))
        dprobs = dot(v, g, NT_DIMS)
        delta = jnp.sum(probs * dprobs, axis=0, keepdims=True)
        dscores = probs * (dprobs - delta) * SCALE
        probs_b = probs.astype(jnp.bfloat16)
        dscores_b = dscores.astype(jnp.bfloat16)
        key_grad = dot(dscores_b, q, NN_DIMS)
        value_grad = dot(probs_b, g, NN_DIMS)
        own_ref[0, :, feats] = key_grad[rows:]
        own_ref[1, :, feats] = value_grad[rows:]
        for which, grad in ((0, key_grad), (1, value_grad)):
            leaving = grad[:rows].astype(jnp.bfloat16)
            if passed:
                leaving = jnp.where(lax.axis_index("ctx") == 0, passed[which][:, feats], leaving)
            other_ref[which, :, feats] = leaving
        if packed:
            bound = rows // 2
            same = same_ref[...] > 0.5
            span = pl.ds(u * lanes, lanes)
            for which, value in ((0, probs), (1, dscores)):
                near = folded(jnp.where(same, value, 0.0), bound)
                far = folded(jnp.where(same, 0.0, value), bound)
                pack_ref[which, :, span] = jnp.concatenate([near, far], axis=0).astype(jnp.bfloat16)
        else:
            attn_ref[:, wide] = spread_heads(dot(probs_b, v, TN_DIMS), rows).astype(jnp.bfloat16)
            gq_ref[:, wide] = spread_heads(dot(dscores_b, k, TN_DIMS), rows).astype(jnp.bfloat16)


def attention(packed, first_slot, slots, q, g, k, v, first_k, first_v, lengths, tiles, passed=()):
    rows = q.shape[1]
    lanes = GROUP_RATIO * rows
    wide = GROUPS_PER_STEP * GROUP_RATIO * HEAD_SIZE
    feats = GROUPS_PER_STEP * HEAD_SIZE
    of_q = pl.BlockSpec((None, rows, wide), lambda s, i: (s + first_slot, 0, i))
    of_k = pl.BlockSpec((None, rows, feats), lambda s, i: (s + first_slot, 0, i))
    of_kv = pl.BlockSpec((None, 2, rows, feats), lambda s, i: (s, 0, 0, i))

    def at(start):
        return pl.BlockSpec((None, rows, feats), lambda s, i: (s + start, 0, i))

    smem = pl.BlockSpec(memory_space=pltpu.SMEM)
    partial = (slots, 2, rows, KEY_VALUE_HEADS * HEAD_SIZE)
    out_shape = [jax.ShapeDtypeStruct(partial, jnp.float32), jax.ShapeDtypeStruct(partial, jnp.bfloat16)]
    out_specs = [of_kv, of_kv]
    scratch = [pltpu.VMEM((2 * rows, lanes), jnp.float32)]
    if packed:
        out_shape.insert(0, jax.ShapeDtypeStruct((2, rows, KEY_VALUE_HEADS * lanes), jnp.bfloat16))
        out_specs.insert(0, pl.BlockSpec((2, rows, GROUPS_PER_STEP * lanes), lambda s, i: (0, 0, i)))
        scratch = scratch * 2
    else:
        out_shape = [pltpu.HBM(q.shape, q.dtype)] * 2 + out_shape
        out_specs = [of_q, of_q] + out_specs
    return pl.pallas_call(
        functools.partial(attention_body, packed, first_slot, rows),
        grid=(slots, KEY_VALUE_HEADS // GROUPS_PER_STEP),
        in_specs=[of_q, of_q, of_k, of_k, at(first_k[1]), at(first_v[1]), smem, smem]
        + [at(start) for _, start in passed],
        out_specs=out_specs,
        out_shape=out_shape,
        scratch_shapes=scratch,
        compiler_params=pltpu.CompilerParams(vmem_limit_bytes=32 * 2**20),
        cost_estimate=CHEAP,
    )(q, g, k, v, first_k[0], first_v[0], lengths, tiles, *[array for array, _ in passed])


def rebuild_body(rows, pack_ref, near_ref, first_ref, zero_ref, lengths_ref, tiles_ref, _a, _b, attn_ref, gq_ref, gk_ref, gv_ref, own_ref, query_ref):
    lanes = GROUP_RATIO * rows
    bound = rows // 2

    @pl.when(pl.program_id(0) == 0)
    def _():
        partner = jnp.bitwise_xor(lax.axis_index("dp"), lax.axis_size("dp") // 2)
        _, own, query = masks(lengths_ref, tiles_ref, 2 * partner + 1, rows, lanes)
        own_ref[...] = jnp.where(own, 1.0, 0.0)
        query_ref[...] = jnp.where(query, 1.0, 0.0)

    for which, out_ref in ((0, gk_ref), (1, gv_ref)):
        arrived = jnp.where(lax.axis_index("ctx") == 0, first_ref[which].astype(jnp.float32), 0.0)
        total = zero_ref[which] + arrived
        out_ref[...] = total.astype(jnp.bfloat16)
    for u in range(GROUPS_PER_STEP):
        feats = pl.ds(u * HEAD_SIZE, HEAD_SIZE)
        wide = pl.ds(u * GROUP_RATIO * HEAD_SIZE, GROUP_RATIO * HEAD_SIZE)
        span = pl.ds(u * lanes, lanes)
        for which, out_ref in ((1, attn_ref), (0, gq_ref)):
            side = jnp.concatenate([first_ref[which, :, feats], near_ref[which, :, feats]], axis=0)
            coded = pack_ref[1 - which, :, span].astype(jnp.float32)
            copies = 2 * rows // bound
            near = jnp.concatenate([coded[:bound]] * copies, axis=0)
            far = jnp.concatenate([coded[bound:]] * copies, axis=0)
            value = jnp.where(own_ref[...] > 0.5, near, jnp.where(query_ref[...] > 0.5, far, 0.0))
            out = dot(value.astype(jnp.bfloat16), side, TN_DIMS)
            out_ref[:, wide] = spread_heads(out, rows).astype(jnp.bfloat16)


def rebuild(pack, kv_near, arrived, own_zero, lengths, tiles, attn, gq):
    rows = attn.shape[1]
    lanes = GROUP_RATIO * rows
    wide = GROUPS_PER_STEP * GROUP_RATIO * HEAD_SIZE
    feats = GROUPS_PER_STEP * HEAD_SIZE
    of_kv = pl.BlockSpec((2, rows, feats), lambda i: (0, 0, i))
    of_q = pl.BlockSpec((None, rows, wide), lambda i: (1, 0, i))
    of_zero = pl.BlockSpec((None, rows, feats), lambda i: (0, 0, i))
    smem = pl.BlockSpec(memory_space=pltpu.SMEM)
    anywhere = pl.BlockSpec(memory_space=pl.ANY)
    return pl.pallas_call(
        functools.partial(rebuild_body, rows),
        grid=(KEY_VALUE_HEADS // GROUPS_PER_STEP,),
        in_specs=[
            pl.BlockSpec((2, rows, GROUPS_PER_STEP * lanes), lambda i: (0, 0, i)),
            of_kv,
            of_kv,
            of_kv,
            smem,
            smem,
            anywhere,
            anywhere,
        ],
        out_specs=[of_q, of_q, of_zero, of_zero],
        out_shape=[pltpu.HBM(attn.shape, attn.dtype)] * 2 + [pltpu.HBM(kv_near.shape, kv_near.dtype)] * 2,
        scratch_shapes=[pltpu.VMEM((2 * rows, lanes), jnp.float32)] * 2,
        input_output_aliases={6: 0, 7: 1},
        compiler_params=pltpu.CompilerParams(vmem_limit_bytes=32 * 2**20),
        cost_estimate=CHEAP,
    )(pack, kv_near, arrived, own_zero, lengths, tiles, attn, gq)


def cut_body(flags_ref, k_ref, v_ref, flag_ref, second_ref):
    flag_ref[0] = flags_ref[lax.axis_index("dp")]
    second_ref[0] = k_ref[...]
    second_ref[1] = v_ref[...]


def cut(flags, k, v):
    smem = pl.BlockSpec(memory_space=pltpu.SMEM)
    second = pl.BlockSpec((None, *k.shape[1:]), lambda i: (1, 0, 0))
    return pl.pallas_call(
        cut_body,
        grid=(1,),
        in_specs=[smem, second, second],
        out_specs=[smem, pl.BlockSpec(k.shape, lambda i: (0, 0, 0))],
        out_shape=[jax.ShapeDtypeStruct((1,), jnp.int32), pltpu.HBM(k.shape, k.dtype)],
        cost_estimate=CHEAP,
    )(flags, k, v)


def finish_body(partner_ref, _a, _b, gk_ref, gv_ref):
    gk_ref[...] = partner_ref[0]
    gv_ref[...] = partner_ref[1]


def finish(grads_partner, gk, gv):
    anywhere = pl.BlockSpec(memory_space=pl.ANY)
    second = pl.BlockSpec((None, *gk.shape[1:]), lambda i: (1, 0, 0))
    return pl.pallas_call(
        finish_body,
        grid=(1,),
        in_specs=[pl.BlockSpec(gk.shape, lambda i: (0, 0, 0)), anywhere, anywhere],
        out_specs=[second, second],
        out_shape=[pltpu.HBM(gk.shape, gk.dtype)] * 2,
        input_output_aliases={1: 0, 2: 1},
        cost_estimate=CHEAP,
    )(grads_partner, gk, gv)


def to_next(value):
    return lax.ppermute(value, "ctx", [(0, 1)])


def to_owner(value):
    return lax.ppermute(value, "ctx", [(1, 0)])


def swapped(value):
    return lax.ppermute(value, "ctx", [(0, 1), (1, 0)])


def to_partner(value):
    size = lax.axis_size("dp")
    return lax.ppermute(value, "dp", [(s, s ^ (size // 2)) for s in range(size)])


def joined(own, arrived):
    return (own + arrived.astype(jnp.float32)).astype(jnp.bfloat16)


def stay(q, k, v, g, lengths, tiles, kv_second):
    first_k, first_v = to_next(k), to_next(v)
    attn, gq, own, other = attention(
        False, 0, 2, q, g, k, v, (first_k, 0), (first_v, 0), lengths, tiles
    )
    grads = joined(own, to_owner(other))
    return attn, gq, grads[:, 0], grads[:, 1]


def trade(q, k, v, g, lengths, tiles, kv_second):
    arrived = swapped(kv_second)
    kv_partner = to_partner(kv_second)
    pack, own_second, leaving = attention(
        True, 1, 1, q, g, k, v, (arrived, 0), (arrived, 1), lengths, tiles, [(k, 0), (v, 0)]
    )
    pack_partner = to_partner(pack)
    arrived = swapped(leaving[0])
    grads_partner = to_partner(joined(own_second[0], jnp.where(lax.axis_index("ctx") == 0, arrived, 0)))
    attn, gq, own_zero, leaving = attention(
        False, 0, 1, q, g, k, v, (arrived, 0), (arrived, 1), lengths, tiles, [(kv_partner, 0), (kv_partner, 1)]
    )
    arrived = swapped(leaving[0])
    attn, gq, gk, gv = rebuild(
        pack_partner, kv_partner, arrived, own_zero[0], lengths, tiles, attn, gq
    )
    return attn, gq, *finish(grads_partner, gk, gv)


def two_rank_shards(query_proj, key_proj, value_proj, grad_attn, doc_lengths, mask_tiles, pair_flags):
    flag, kv_second = cut(pair_flags, key_proj, value_proj)
    return lax.cond(
        flag[0] == 1,
        trade,
        stay,
        query_proj,
        key_proj,
        value_proj,
        grad_attn,
        doc_lengths.T,
        mask_tiles.transpose(1, 2, 0),
        kv_second,
    )


def from_partner(value, axis, distance):
    mask = 2**distance
    pairs = [(source, source ^ mask) for source in range(lax.axis_size(axis))]
    return lax.ppermute(value, axis, pairs)


def sequence_core(
    query_rows, sequence_keys, sequence_values, sequence_gradients, lengths, tile_table, row_start
):
    rows = query_rows.shape[0]
    length_total = sequence_keys.shape[0]
    groups = sequence_keys.shape[1] // HEAD_SIZE
    group_ratio = QUERY_HEADS // KEY_VALUE_HEADS
    scale = HEAD_SIZE ** (-0.5)
    row_pos = row_start + jnp.arange(rows, dtype=jnp.int32)
    col_pos = jnp.arange(length_total, dtype=jnp.int32)
    ends = jnp.cumsum(lengths)[:-1]
    row_doc = jnp.sum((row_pos[:, None] >= ends[None, :]).astype(jnp.int32), axis=1)
    col_doc = jnp.sum((col_pos[:, None] >= ends[None, :]).astype(jnp.int32), axis=1)
    tile_count = tile_table.shape[0]
    tile_len = length_total // tile_count
    tile_ids = jnp.arange(tile_count, dtype=jnp.int32)
    row_pick = ((row_pos // tile_len)[:, None] == tile_ids[None, :]).astype(jnp.float32)
    col_pick = ((col_pos // tile_len)[:, None] == tile_ids[None, :]).astype(jnp.float32)
    tile_map = jnp.dot(jnp.dot(row_pick, tile_table.astype(jnp.float32)), col_pick.T) > 0.5
    allowed = (
        (col_pos[None, :] <= row_pos[:, None])
        & ((col_doc[None, :] == row_doc[:, None]) | (col_doc[None, :] == 0))
        & tile_map
    )
    heads_of_queries = query_rows.reshape(rows, groups, group_ratio, HEAD_SIZE)
    heads_of_keys = sequence_keys.reshape(length_total, groups, HEAD_SIZE)
    heads_of_values = sequence_values.reshape(length_total, groups, HEAD_SIZE)
    head_gradients = sequence_gradients.reshape(rows, groups, group_ratio, HEAD_SIZE)
    scores = (
        jnp.einsum(
            "igrd,jgd->grij", heads_of_queries, heads_of_keys, preferred_element_type=jnp.float32
        )
        * scale
    )
    scores = jnp.where(allowed, scores, -1e30)
    peak = jnp.max(scores, axis=-1, keepdims=True)
    expd = jnp.where(allowed, jnp.exp(scores - peak), 0.0)
    probs = expd / jnp.sum(expd, axis=-1, keepdims=True)
    probs_b = probs.astype(jnp.bfloat16)
    attn = jnp.einsum(
        "grij,jgd->igrd", probs_b, heads_of_values, preferred_element_type=jnp.float32
    ).astype(jnp.bfloat16)
    delta = jnp.transpose(
        jnp.sum(head_gradients.astype(jnp.float32) * attn.astype(jnp.float32), axis=-1), (1, 2, 0)
    )
    value_gradient = jnp.einsum(
        "grij,igrd->jgd", probs_b, head_gradients, preferred_element_type=jnp.float32
    )
    dprobs = jnp.einsum(
        "igrd,jgd->grij", head_gradients, heads_of_values, preferred_element_type=jnp.float32
    )
    dscores = (probs * (dprobs - delta[..., None]) * scale).astype(jnp.bfloat16)
    grad_q = jnp.einsum(
        "grij,jgd->igrd", dscores, heads_of_keys, preferred_element_type=jnp.float32
    )
    key_gradient = jnp.einsum(
        "grij,igrd->jgd", dscores, heads_of_queries, preferred_element_type=jnp.float32
    )
    return (
        attn.reshape(rows, -1),
        grad_q.astype(jnp.bfloat16).reshape(rows, -1),
        key_gradient.reshape(length_total, -1),
        value_gradient.reshape(length_total, -1),
    )


def attend(query_rows, keys_in, values_in, grads_in, lengths_all, tiles_all, first_id, second_id):
    seq_ids = jnp.stack([first_id, second_id])
    lengths_pair = jnp.take(lengths_all, seq_ids, axis=0)
    tiles_pair = jnp.take(tiles_all, seq_ids, axis=0)
    ctx_rank = lax.axis_index("ctx")
    seq_dev = query_rows.shape[1]
    keys_all, values_all = (
        lax.all_gather(keys_in, "ctx", axis=1, tiled=True),
        lax.all_gather(values_in, "ctx", axis=1, tiled=True),
    )
    pieces = [
        sequence_core(
            query_rows[seq_slot],
            keys_all[seq_slot],
            values_all[seq_slot],
            grads_in[seq_slot],
            lengths_pair[seq_slot],
            tiles_pair[seq_slot],
            ctx_rank * seq_dev,
        )
        for seq_slot in range(2)
    ]
    attn = jnp.stack([pieces[0][0], pieces[1][0]])
    grad_q = jnp.stack([pieces[0][1], pieces[1][1]])
    key_terms = jnp.stack([pieces[0][2], pieces[1][2]])
    value_terms = jnp.stack([pieces[0][3], pieces[1][3]])
    key_sums, value_sums = (
        lax.psum_scatter(key_terms, "ctx", scatter_dimension=1, tiled=True),
        lax.psum_scatter(value_terms, "ctx", scatter_dimension=1, tiled=True),
    )
    return (attn, grad_q, key_sums.astype(jnp.bfloat16), value_sums.astype(jnp.bfloat16))


def take_second(mine, arrived, swapped):
    return jnp.stack([mine[0], jnp.where(swapped, arrived, mine[1])])


def shards(query_proj, key_proj, value_proj, grad_attn, doc_lengths, mask_tiles, pair_flags):
    dp_size = lax.axis_size("dp")
    dp_rank = lax.axis_index("dp")
    far_bit = dp_size.bit_length() - 2
    partner = jnp.bitwise_xor(dp_rank, dp_size // 2)
    pair_flag = lax.dynamic_index_in_dim(pair_flags, dp_rank, 0, keepdims=False)
    swapped = pair_flag == 1
    first_id = 2 * dp_rank
    second_id = jnp.where(swapped, 2 * partner + 1, 2 * dp_rank + 1)
    arrived = from_partner((query_proj[1], key_proj[1], value_proj[1], grad_attn[1]), "dp", far_bit)
    query_now = take_second(query_proj, arrived[0], swapped)
    key_now = take_second(key_proj, arrived[1], swapped)
    value_now = take_second(value_proj, arrived[2], swapped)
    grad_now = take_second(grad_attn, arrived[3], swapped)
    return attend(
        query_now, key_now, value_now, grad_now, doc_lengths, mask_tiles, first_id, second_id
    )


def solution(mesh):
    in_specs = (
        P("dp", "ctx", None),
        P("dp", "ctx", None),
        P("dp", "ctx", None),
        P("dp", "ctx", None),
        P(),
        P(),
        P(),
    )
    out_specs = (
        P("dp", "ctx", None),
        P("dp", "ctx", None),
        P("dp", "ctx", None),
        P("dp", "ctx", None),
    )
    form = two_rank_shards if mesh.shape["ctx"] == 2 else shards
    return jax.shard_map(form, mesh=mesh, in_specs=in_specs, out_specs=out_specs, check_vma=False)
```

```python
import functools

import jax
import jax.numpy as jnp
from jax import lax
from jax.experimental import pallas as pl
from jax.experimental.pallas import tpu as pltpu
from jax.sharding import PartitionSpec as P

QUERY_HEADS = 32
KEY_VALUE_HEADS = 8
HEAD_SIZE = 128
GROUP_RATIO = QUERY_HEADS // KEY_VALUE_HEADS
SCALE = HEAD_SIZE ** (-0.5)
NDOC = 8
PARAMS = pltpu.CompilerParams(vmem_limit_bytes=32 * 2**20)
LONG = pl.CostEstimate(flops=1, bytes_accessed=2**27, transcendentals=0)
CHEAP = pl.CostEstimate(flops=1, bytes_accessed=1, transcendentals=0)
NT_DIMS = (((1,), (1,)), ((), ()))
TN_DIMS = (((0,), (0,)), ((), ()))
NN_DIMS = (((1,), (0,)), ((), ()))


def dot(a, b, dims):
    return lax.dot_general(a, b, dims, preferred_element_type=jnp.float32)


def masks(facts_ref, which, rows, lanes):
    ctx = lax.axis_index("ctx")
    key_index = lax.broadcasted_iota(jnp.int32, (2 * rows, lanes), 0)
    lane = lax.broadcasted_iota(jnp.int32, (2 * rows, lanes), 1)
    col_pos = key_index + (ctx - 1) * rows
    row_pos = lax.rem(lane, rows) + ctx * rows
    col_doc = jnp.zeros_like(col_pos)
    row_doc = jnp.zeros_like(row_pos)
    for d in range(NDOC - 1):
        end = facts_ref[which * NDOC + d]
        col_doc = col_doc + (col_pos >= end).astype(jnp.int32)
        row_doc = row_doc + (row_pos >= end).astype(jnp.int32)
    seen = (key_index >= rows) | (facts_ref[which * NDOC + NDOC - 1] == 1)
    own = (col_doc == row_doc) & (col_pos >= 0)
    query = (col_doc == 0) & (col_pos >= 0)
    allowed = (col_pos <= row_pos) & (own | query) & seen
    recent = own & (row_pos >= col_pos) & (row_pos - col_pos < rows // 4)
    older = own & (row_pos - col_pos >= rows // 4)
    return allowed, recent, older, query & jnp.logical_not(own)


def as_factor(mask):
    return jnp.where(mask, 1.0, 0.0).astype(jnp.bfloat16)


def pairing(rows, lanes):
    window = rows // 4
    lane = lax.broadcasted_iota(jnp.int32, (lanes, lanes // 2), 0)
    shared = lax.broadcasted_iota(jnp.int32, (lanes, lanes // 2), 1)
    target = lane // (2 * window) * window + lax.rem(lane, window)
    return as_factor(target == shared)


def stacked_heads(block, rows):
    return jnp.concatenate(
        [block[:, h * HEAD_SIZE : (h + 1) * HEAD_SIZE] for h in range(GROUP_RATIO)], axis=0
    )


def spread_heads(value, rows):
    return jnp.concatenate([value[h * rows : (h + 1) * rows] for h in range(GROUP_RATIO)], axis=1)


def folded(value, bound):
    total = value[:bound]
    for b in range(1, value.shape[0] // bound):
        total = total + value[b * bound : (b + 1) * bound]
    return total


def attention_body(
    far, first_slot, rows, q_ref, g_ref, k_ref, v_ref, kf_ref, vf_ref, facts_ref, *rest
):
    lanes = GROUP_RATIO * rows
    window = rows // 4
    if far:
        *passed, pack_ref, own_ref, other_ref, bias_ref, recent_ref, older_ref, far_ref = rest
    else:
        *passed, attn_ref, gq_ref, own_ref, other_ref, bias_ref = rest
    allowed, recent, older, query = masks(facts_ref, first_slot + pl.program_id(0), rows, lanes)
    bias_ref[...] = jnp.where(allowed, 0.0, -1e30)
    if far:
        recent_ref[...] = as_factor(recent)
        older_ref[...] = as_factor(older)
        far_ref[...] = as_factor(query)

    units = range(k_ref.shape[1] // HEAD_SIZE)
    feats = [pl.ds(u * HEAD_SIZE, HEAD_SIZE) for u in units]
    wide = [pl.ds(u * GROUP_RATIO * HEAD_SIZE, GROUP_RATIO * HEAD_SIZE) for u in units]
    q = [stacked_heads(q_ref[:, wide[u]], rows) for u in units]
    g = [stacked_heads(g_ref[:, wide[u]], rows) for u in units]
    k = [jnp.concatenate([kf_ref[:, feats[u]], k_ref[:, feats[u]]], axis=0) for u in units]
    v = [jnp.concatenate([vf_ref[:, feats[u]], v_ref[:, feats[u]]], axis=0) for u in units]
    scores = [dot(k[u], q[u], NT_DIMS) for u in units]
    dprobs = [dot(v[u], g[u], NT_DIMS) for u in units]
    bias = bias_ref[...]
    scores = [scores[u] * SCALE + bias for u in units]
    peak = [jnp.max(scores[u], axis=0, keepdims=True) for u in units]
    expd = [jnp.exp(scores[u] - peak[u]) for u in units]
    inverse = [1.0 / jnp.sum(expd[u], axis=0, keepdims=True) for u in units]
    probs = [expd[u] * inverse[u] for u in units]
    delta = [jnp.sum(probs[u] * dprobs[u], axis=0, keepdims=True) for u in units]
    dscores = [probs[u] * ((dprobs[u] - delta[u]) * SCALE) for u in units]
    probs = [probs[u].astype(jnp.bfloat16) for u in units]
    dscores = [dscores[u].astype(jnp.bfloat16) for u in units]
    if far:
        shared = []
        for which, values in ((0, probs), (1, dscores)):
            top = which * (far + window)
            for u in units:
                span = pl.ds(u * lanes, lanes)
                pack_ref[top : top + far, span] = folded(values[u] * far_ref[...], far)
                pack_ref[top + far : top + far + window, span] = folded(values[u] * recent_ref[...], window)
                shared.append(folded(values[u] * older_ref[...], window))
        shared = dot(jnp.concatenate(shared, axis=0), pairing(rows, lanes), NN_DIMS).astype(jnp.bfloat16)
        for n in range(2 * KEY_VALUE_HEADS):
            span = pl.ds(n * lanes // 2, lanes // 2)
            pack_ref[2 * (far + window) :, span] = shared[n * window : (n + 1) * window]
    key_grad = [dot(dscores[u], q[u], NN_DIMS) for u in units]
    value_grad = [dot(probs[u], g[u], NN_DIMS) for u in units]
    for u in units:
        for which, grad in ((0, key_grad[u]), (1, value_grad[u])):
            own_ref[which, :, feats[u]] = grad[rows:]
            leaving = grad[:rows].astype(jnp.bfloat16)
            if passed:
                leaving = jnp.where(lax.axis_index("ctx") == 0, passed[which][:, feats[u]], leaving)
            other_ref[which, :, feats[u]] = leaving
    if not far:
        for u in units:
            out = dot(probs[u], v[u], TN_DIMS)
            attn_ref[:, wide[u]] = spread_heads(out, rows).astype(jnp.bfloat16)
            out = dot(dscores[u], k[u], TN_DIMS)
            gq_ref[:, wide[u]] = spread_heads(out, rows).astype(jnp.bfloat16)


def attention(far, first_slot, slots, q, g, k, v, first_k, first_v, facts, passed=()):
    rows = q.shape[1]
    lanes = GROUP_RATIO * rows

    def at(array, start):
        return pl.BlockSpec((None, *array.shape[1:]), lambda s: (s + start, 0, 0))

    of_q = at(q, first_slot)
    partial = (slots, 2, *k.shape[1:])
    of_partial = pl.BlockSpec((None, *partial[1:]), lambda s: (s, 0, 0, 0))
    smem = pl.BlockSpec(memory_space=pltpu.SMEM)
    out_shape = [jax.ShapeDtypeStruct(partial, jnp.float32), jax.ShapeDtypeStruct(partial, jnp.bfloat16)]
    out_specs = [of_partial, of_partial]
    scratch = [pltpu.VMEM((2 * rows, lanes), jnp.float32)]
    if far:
        coded = (2 * far + 3 * rows // 4, KEY_VALUE_HEADS * lanes)
        out_shape.insert(0, jax.ShapeDtypeStruct(coded, jnp.bfloat16))
        out_specs.insert(0, pl.BlockSpec(coded, lambda s: (0, 0)))
        scratch += [pltpu.VMEM((2 * rows, lanes), jnp.bfloat16)] * 3
    else:
        out_shape = [pltpu.HBM(q.shape, q.dtype)] * 2 + out_shape
        out_specs = [of_q, of_q] + out_specs
    return pl.pallas_call(
        functools.partial(attention_body, far, first_slot, rows),
        grid=(slots,),
        in_specs=[of_q, of_q, at(k, first_slot), at(v, first_slot), at(*first_k), at(*first_v), smem]
        + [at(*array) for array in passed],
        out_specs=out_specs,
        out_shape=out_shape,
        scratch_shapes=scratch,
        compiler_params=PARAMS,
        cost_estimate=CHEAP,
    )(q, g, k, v, first_k[0], first_v[0], facts, *[array for array, _ in passed])


def rebuild_body(
    far, rows, pack_ref, near_ref, first_ref, zero_ref, facts_ref, _a, _b, attn_ref, gq_ref, gk_ref, gv_ref
):
    lanes = GROUP_RATIO * rows
    window = rows // 4
    _, recent, older, query = masks(facts_ref, 2, rows, lanes)
    recent, older, query = as_factor(recent), as_factor(older), as_factor(query)
    for which, out_ref in ((0, gk_ref), (1, gv_ref)):
        arrived = jnp.where(lax.axis_index("ctx") == 0, first_ref[which].astype(jnp.float32), 0.0)
        out_ref[...] = (zero_ref[which] + arrived).astype(jnp.bfloat16)
    shared = [
        pack_ref[2 * (far + window) :, pl.ds(n * lanes // 2, lanes // 2)]
        for n in range(2 * KEY_VALUE_HEADS)
    ]
    shared = dot(jnp.concatenate(shared, axis=0), pairing(rows, lanes), NT_DIMS).astype(jnp.bfloat16)

    def spread(part):
        return jnp.concatenate([part] * (2 * rows // part.shape[0]), axis=0)

    for which, side_index, out_ref in ((0, 1, attn_ref), (1, 0, gq_ref)):
        top = which * (far + window)
        for u in range(KEY_VALUE_HEADS):
            feats = pl.ds(u * HEAD_SIZE, HEAD_SIZE)
            wide = pl.ds(u * GROUP_RATIO * HEAD_SIZE, GROUP_RATIO * HEAD_SIZE)
            span = pl.ds(u * lanes, lanes)
            side = jnp.concatenate([first_ref[side_index, :, feats], near_ref[side_index, :, feats]], axis=0)
            n = which * KEY_VALUE_HEADS + u
            value = spread(pack_ref[top : top + far, span]) * query
            value += spread(pack_ref[top + far : top + far + window, span]) * recent
            value += spread(shared[n * window : (n + 1) * window]) * older
            out_ref[:, wide] = spread_heads(dot(value, side, TN_DIMS), rows).astype(jnp.bfloat16)


def rebuild(far, pack, kv_near, arrived, own_zero, facts, attn, gq):
    rows = attn.shape[1]

    def whole(array):
        return pl.BlockSpec(array.shape, lambda i: (0,) * array.ndim)

    def at(array, slot):
        return pl.BlockSpec((None, *array.shape[1:]), lambda i: (slot, 0, 0))

    smem = pl.BlockSpec(memory_space=pltpu.SMEM)
    anywhere = pl.BlockSpec(memory_space=pl.ANY)
    return pl.pallas_call(
        functools.partial(rebuild_body, far, rows),
        grid=(1,),
        in_specs=[whole(x) for x in (pack, kv_near, arrived, own_zero)] + [smem, anywhere, anywhere],
        out_specs=[at(attn, 1), at(gq, 1), at(kv_near, 0), at(kv_near, 0)],
        out_shape=[pltpu.HBM(attn.shape, attn.dtype)] * 2 + [pltpu.HBM(kv_near.shape, kv_near.dtype)] * 2,
        input_output_aliases={5: 0, 6: 1},
        compiler_params=PARAMS,
        cost_estimate=LONG,
    )(pack, kv_near, arrived, own_zero, facts, attn, gq)


def cut_body(
    flags_in, lengths_in, tiles_in, k_ref, v_ref,
    form_ref, facts_ref, second_ref,
    flags_ref, lengths_ref, tiles_ref, scalar_sems, sems,
):
    scalars = ((flags_in, flags_ref), (lengths_in, lengths_ref), (tiles_in, tiles_ref))
    scalars = [pltpu.make_async_copy(a, b, scalar_sems.at[i]) for i, (a, b) in enumerate(scalars)]
    copies = [
        pltpu.make_async_copy(ref.at[1], second_ref.at[i], sems.at[i])
        for i, ref in enumerate((k_ref, v_ref))
    ]
    for copy in scalars + copies:
        copy.start()
    for copy in scalars:
        copy.wait()
    rank = lax.axis_index("dp")
    ctx = lax.axis_index("ctx")
    partner = jnp.bitwise_xor(rank, lax.axis_size("dp") // 2)
    longest = jnp.maximum(lengths_ref[0, 2 * rank + 1], lengths_ref[0, 2 * partner + 1])
    form_ref[0] = flags_ref[rank] * jnp.where(longest > k_ref.shape[1] // 4, 2, 1)
    for which, seq in enumerate((2 * rank, 2 * rank + 1, 2 * partner + 1)):
        end = jnp.int32(0)
        for d in range(NDOC - 1):
            end = end + lengths_ref[d, seq]
            facts_ref[which * NDOC + d] = end
        facts_ref[which * NDOC + NDOC - 1] = tiles_ref[ctx, 0, seq]
    for copy in copies:
        copy.wait()


def cut(flags, lengths, tiles, k, v):
    smem = pl.BlockSpec(memory_space=pltpu.SMEM)
    vmem = pl.BlockSpec(memory_space=pltpu.VMEM)
    anywhere = pl.BlockSpec(memory_space=pl.ANY)
    whole = jax.ShapeDtypeStruct(k.shape, k.dtype)
    return pl.pallas_call(
        cut_body,
        in_specs=[anywhere] * 5,
        out_specs=[smem, smem, vmem],
        out_shape=[
            jax.ShapeDtypeStruct((1,), jnp.int32),
            jax.ShapeDtypeStruct((3 * NDOC,), jnp.int32),
            whole,
        ],
        scratch_shapes=[pltpu.SMEM(x.shape, x.dtype) for x in (flags, lengths, tiles)]
        + [pltpu.SemaphoreType.DMA((3,)), pltpu.SemaphoreType.DMA((2,))],
        cost_estimate=CHEAP,
    )(flags, lengths, tiles, k, v)


def finish_body(partner_ref, _a, _b, gk_ref, gv_ref):
    gk_ref[...] = partner_ref[0]
    gv_ref[...] = partner_ref[1]


def finish(grads_partner, gk, gv):
    anywhere = pl.BlockSpec(memory_space=pl.ANY)
    second = pl.BlockSpec((None, *gk.shape[1:]), lambda i: (1, 0, 0))
    return pl.pallas_call(
        finish_body,
        grid=(1,),
        in_specs=[pl.BlockSpec(gk.shape, lambda i: (0, 0, 0)), anywhere, anywhere],
        out_specs=[second, second],
        out_shape=[pltpu.HBM(gk.shape, gk.dtype)] * 2,
        input_output_aliases={1: 0, 2: 1},
        compiler_params=PARAMS,
        cost_estimate=CHEAP,
    )(grads_partner, gk, gv)


def to_next(value):
    return lax.ppermute(value, "ctx", [(0, 1)])


def to_owner(value):
    return lax.ppermute(value, "ctx", [(1, 0)])


def swapped(value):
    return lax.ppermute(value, "ctx", [(0, 1), (1, 0)])


def to_partner(value):
    size = lax.axis_size("dp")
    return lax.ppermute(value, "dp", [(s, s ^ (size // 2)) for s in range(size)])


def joined(own, arrived):
    return (own + arrived.astype(jnp.float32)).astype(jnp.bfloat16)


def stay(q, k, v, g, facts, second):
    first_k = swapped(k)
    v_later, first_k = lax.optimization_barrier((v, first_k))
    first_v = swapped(v_later)
    attn, gq, own, leaving = attention(0, 0, 2, q, g, k, v, (first_k, 0), (first_v, 0), facts)
    arrived = swapped(leaving)
    grads = joined(own, jnp.where(lax.axis_index("ctx") == 0, arrived, 0))
    return attn, gq, grads[:, 0], grads[:, 1]


def trade(far, q, k, v, g, facts, second):
    arrived = swapped(second)
    kv_partner = to_partner(second)
    pack, own_second, leaving = attention(
        far, 1, 1, q, g, k, v, (arrived, 0), (arrived, 1), facts, [(k, 0), (v, 0)]
    )
    arrived = swapped(leaving[0])
    pack_partner = to_partner(pack)
    grads = joined(own_second[0], jnp.where(lax.axis_index("ctx") == 0, arrived, 0))
    grads_partner = to_partner(grads)
    attn, gq, own_zero, leaving = attention(
        0, 0, 1, q, g, k, v, (arrived, 0), (arrived, 1), facts, [(kv_partner, 0), (kv_partner, 1)]
    )
    arrived = swapped(leaving[0])
    attn, gq, gk, gv = rebuild(far, pack_partner, kv_partner, arrived, own_zero[0], facts, attn, gq)
    return attn, gq, *finish(grads_partner, gk, gv)


def two_rank_shards(query_proj, key_proj, value_proj, grad_attn, doc_lengths, mask_tiles, pair_flags):
    rows = query_proj.shape[1]
    form, *cuts = cut(
        pair_flags, doc_lengths.T, mask_tiles.transpose(1, 2, 0), key_proj, value_proj
    )
    forms = (stay, functools.partial(trade, rows // 4), functools.partial(trade, rows // 2))
    return lax.switch(form[0], forms, query_proj, key_proj, value_proj, grad_attn, *cuts)


def from_partner(value, axis, distance):
    mask = 2**distance
    pairs = [(source, source ^ mask) for source in range(lax.axis_size(axis))]
    return lax.ppermute(value, axis, pairs)


def sequence_core(
    query_rows, sequence_keys, sequence_values, sequence_gradients, lengths, tile_table, row_start
):
    rows = query_rows.shape[0]
    length_total = sequence_keys.shape[0]
    groups = sequence_keys.shape[1] // HEAD_SIZE
    group_ratio = QUERY_HEADS // KEY_VALUE_HEADS
    scale = HEAD_SIZE ** (-0.5)
    row_pos = row_start + jnp.arange(rows, dtype=jnp.int32)
    col_pos = jnp.arange(length_total, dtype=jnp.int32)
    ends = jnp.cumsum(lengths)[:-1]
    row_doc = jnp.sum((row_pos[:, None] >= ends[None, :]).astype(jnp.int32), axis=1)
    col_doc = jnp.sum((col_pos[:, None] >= ends[None, :]).astype(jnp.int32), axis=1)
    tile_count = tile_table.shape[0]
    tile_len = length_total // tile_count
    tile_ids = jnp.arange(tile_count, dtype=jnp.int32)
    row_pick = ((row_pos // tile_len)[:, None] == tile_ids[None, :]).astype(jnp.float32)
    col_pick = ((col_pos // tile_len)[:, None] == tile_ids[None, :]).astype(jnp.float32)
    tile_map = jnp.dot(jnp.dot(row_pick, tile_table.astype(jnp.float32)), col_pick.T) > 0.5
    allowed = (
        (col_pos[None, :] <= row_pos[:, None])
        & ((col_doc[None, :] == row_doc[:, None]) | (col_doc[None, :] == 0))
        & tile_map
    )
    heads_of_queries = query_rows.reshape(rows, groups, group_ratio, HEAD_SIZE)
    heads_of_keys = sequence_keys.reshape(length_total, groups, HEAD_SIZE)
    heads_of_values = sequence_values.reshape(length_total, groups, HEAD_SIZE)
    head_gradients = sequence_gradients.reshape(rows, groups, group_ratio, HEAD_SIZE)
    scores = (
        jnp.einsum(
            "igrd,jgd->grij", heads_of_queries, heads_of_keys, preferred_element_type=jnp.float32
        )
        * scale
    )
    scores = jnp.where(allowed, scores, -1e30)
    peak = jnp.max(scores, axis=-1, keepdims=True)
    expd = jnp.where(allowed, jnp.exp(scores - peak), 0.0)
    probs = expd / jnp.sum(expd, axis=-1, keepdims=True)
    probs_b = probs.astype(jnp.bfloat16)
    attn = jnp.einsum(
        "grij,jgd->igrd", probs_b, heads_of_values, preferred_element_type=jnp.float32
    ).astype(jnp.bfloat16)
    delta = jnp.transpose(
        jnp.sum(head_gradients.astype(jnp.float32) * attn.astype(jnp.float32), axis=-1), (1, 2, 0)
    )
    value_gradient = jnp.einsum(
        "grij,igrd->jgd", probs_b, head_gradients, preferred_element_type=jnp.float32
    )
    dprobs = jnp.einsum(
        "igrd,jgd->grij", head_gradients, heads_of_values, preferred_element_type=jnp.float32
    )
    dscores = (probs * (dprobs - delta[..., None]) * scale).astype(jnp.bfloat16)
    grad_q = jnp.einsum(
        "grij,jgd->igrd", dscores, heads_of_keys, preferred_element_type=jnp.float32
    )
    key_gradient = jnp.einsum(
        "grij,igrd->jgd", dscores, heads_of_queries, preferred_element_type=jnp.float32
    )
    return (
        attn.reshape(rows, -1),
        grad_q.astype(jnp.bfloat16).reshape(rows, -1),
        key_gradient.reshape(length_total, -1),
        value_gradient.reshape(length_total, -1),
    )


def attend(query_rows, keys_in, values_in, grads_in, lengths_all, tiles_all, first_id, second_id):
    seq_ids = jnp.stack([first_id, second_id])
    lengths_pair = jnp.take(lengths_all, seq_ids, axis=0)
    tiles_pair = jnp.take(tiles_all, seq_ids, axis=0)
    ctx_rank = lax.axis_index("ctx")
    seq_dev = query_rows.shape[1]
    keys_all, values_all = (
        lax.all_gather(keys_in, "ctx", axis=1, tiled=True),
        lax.all_gather(values_in, "ctx", axis=1, tiled=True),
    )
    pieces = [
        sequence_core(
            query_rows[seq_slot],
            keys_all[seq_slot],
            values_all[seq_slot],
            grads_in[seq_slot],
            lengths_pair[seq_slot],
            tiles_pair[seq_slot],
            ctx_rank * seq_dev,
        )
        for seq_slot in range(2)
    ]
    attn = jnp.stack([pieces[0][0], pieces[1][0]])
    grad_q = jnp.stack([pieces[0][1], pieces[1][1]])
    key_terms = jnp.stack([pieces[0][2], pieces[1][2]])
    value_terms = jnp.stack([pieces[0][3], pieces[1][3]])
    key_sums, value_sums = (
        lax.psum_scatter(key_terms, "ctx", scatter_dimension=1, tiled=True),
        lax.psum_scatter(value_terms, "ctx", scatter_dimension=1, tiled=True),
    )
    return (attn, grad_q, key_sums.astype(jnp.bfloat16), value_sums.astype(jnp.bfloat16))


def take_second(mine, arrived, swapped):
    return jnp.stack([mine[0], jnp.where(swapped, arrived, mine[1])])


def shards(query_proj, key_proj, value_proj, grad_attn, doc_lengths, mask_tiles, pair_flags):
    dp_size = lax.axis_size("dp")
    dp_rank = lax.axis_index("dp")
    far_bit = dp_size.bit_length() - 2
    partner = jnp.bitwise_xor(dp_rank, dp_size // 2)
    pair_flag = lax.dynamic_index_in_dim(pair_flags, dp_rank, 0, keepdims=False)
    swapped = pair_flag == 1
    first_id = 2 * dp_rank
    second_id = jnp.where(swapped, 2 * partner + 1, 2 * dp_rank + 1)
    arrived = from_partner((query_proj[1], key_proj[1], value_proj[1], grad_attn[1]), "dp", far_bit)
    query_now = take_second(query_proj, arrived[0], swapped)
    key_now = take_second(key_proj, arrived[1], swapped)
    value_now = take_second(value_proj, arrived[2], swapped)
    grad_now = take_second(grad_attn, arrived[3], swapped)
    return attend(
        query_now, key_now, value_now, grad_now, doc_lengths, mask_tiles, first_id, second_id
    )


def solution(mesh):
    in_specs = (
        P("dp", "ctx", None),
        P("dp", "ctx", None),
        P("dp", "ctx", None),
        P("dp", "ctx", None),
        P(),
        P(),
        P(),
    )
    out_specs = (
        P("dp", "ctx", None),
        P("dp", "ctx", None),
        P("dp", "ctx", None),
        P("dp", "ctx", None),
    )
    form = two_rank_shards if mesh.shape["ctx"] == 2 else shards
    return jax.shard_map(form, mesh=mesh, in_specs=in_specs, out_specs=out_specs, check_vma=False)
```

```python
import functools

import jax
import jax.numpy as jnp
from jax import lax
from jax.experimental import pallas as pl
from jax.experimental.pallas import tpu as pltpu
from jax.sharding import PartitionSpec as P

QUERY_HEADS = 32
KEY_VALUE_HEADS = 8
HEAD_SIZE = 128
GROUP_RATIO = QUERY_HEADS // KEY_VALUE_HEADS
SCALE = HEAD_SIZE ** (-0.5)
NDOC = 8
PARAMS = pltpu.CompilerParams(vmem_limit_bytes=32 * 2**20)
LONG = pl.CostEstimate(flops=1, bytes_accessed=2**27, transcendentals=0)
CHEAP = pl.CostEstimate(flops=1, bytes_accessed=1, transcendentals=0)
NT_DIMS = (((1,), (1,)), ((), ()))
TN_DIMS = (((0,), (0,)), ((), ()))
NN_DIMS = (((1,), (0,)), ((), ()))


def dot(a, b, dims):
    return lax.dot_general(a, b, dims, preferred_element_type=jnp.float32)


def masks(facts_ref, which, rows, lanes):
    ctx = lax.axis_index("ctx")
    key_index = lax.broadcasted_iota(jnp.int32, (2 * rows, 1), 0)
    col_pos = key_index + (ctx - 1) * rows
    row_pos = lax.rem(lax.broadcasted_iota(jnp.int32, (1, lanes), 1), rows) + ctx * rows
    col_doc = jnp.zeros_like(col_pos)
    row_doc = jnp.zeros_like(row_pos)
    for d in range(NDOC - 1):
        end = facts_ref[which * NDOC + d]
        col_doc = col_doc + (col_pos >= end).astype(jnp.int32)
        row_doc = row_doc + (row_pos >= end).astype(jnp.int32)
    seen = (key_index >= rows) | (facts_ref[which * NDOC + NDOC - 1] == 1)
    col_doc = jnp.where(seen & (col_pos >= 0), col_doc, -1)
    back = row_pos - col_pos
    own = (col_doc == row_doc) & (back >= 0)
    query = (col_doc == 0) & (row_doc != 0)
    return own | query, own & (back < rows // 4), own & (back >= rows // 4), query


def as_factor(mask):
    return jnp.where(mask, 1.0, 0.0).astype(jnp.bfloat16)


def pairing(rows, lanes):
    window = rows // 4
    lane = lax.broadcasted_iota(jnp.int32, (lanes, lanes // 2), 0)
    shared = lax.broadcasted_iota(jnp.int32, (lanes, lanes // 2), 1)
    target = lane // (2 * window) * window + lax.rem(lane, window)
    return as_factor(target == shared)


def stacked_heads(block, rows):
    return jnp.concatenate(
        [block[:, h * HEAD_SIZE : (h + 1) * HEAD_SIZE] for h in range(GROUP_RATIO)], axis=0
    )


def spread_heads(value, rows):
    return jnp.concatenate([value[h * rows : (h + 1) * rows] for h in range(GROUP_RATIO)], axis=1)


def folded(value, bound):
    total = value[:bound]
    for b in range(1, value.shape[0] // bound):
        total = total + value[b * bound : (b + 1) * bound]
    return total


def attention_body(
    far, first_slot, rows, q_ref, g_ref, k_ref, v_ref, kf_ref, vf_ref, bias_ref, factors_ref, pairing_ref, *rest
):
    lanes = GROUP_RATIO * rows
    window = rows // 4
    if far:
        *passed, pack_ref, own_ref, other_ref = rest
        recent_ref, older_ref, far_ref = (factors_ref.at[i] for i in range(3))
    else:
        *passed, attn_ref, gq_ref, own_ref, other_ref = rest

    units = range(k_ref.shape[1] // HEAD_SIZE)
    feats = [pl.ds(u * HEAD_SIZE, HEAD_SIZE) for u in units]
    wide = [pl.ds(u * GROUP_RATIO * HEAD_SIZE, GROUP_RATIO * HEAD_SIZE) for u in units]
    q = [stacked_heads(q_ref[:, wide[u]], rows) for u in units]
    g = [stacked_heads(g_ref[:, wide[u]], rows) for u in units]
    k = [jnp.concatenate([kf_ref[:, feats[u]], k_ref[:, feats[u]]], axis=0) for u in units]
    v = [jnp.concatenate([vf_ref[:, feats[u]], v_ref[:, feats[u]]], axis=0) for u in units]
    scores = [dot(k[u], q[u], NT_DIMS) for u in units]
    dprobs = [dot(v[u], g[u], NT_DIMS) for u in units]
    bias = bias_ref[first_slot + pl.program_id(0)]
    scores = [scores[u] * SCALE + bias for u in units]
    peak = [jnp.max(scores[u], axis=0, keepdims=True) for u in units]
    expd = [jnp.exp(scores[u] - peak[u]) for u in units]
    inverse = [1.0 / jnp.sum(expd[u], axis=0, keepdims=True) for u in units]
    probs = [expd[u] * inverse[u] for u in units]
    delta = [jnp.sum(probs[u] * dprobs[u], axis=0, keepdims=True) for u in units]
    dscores = [probs[u] * ((dprobs[u] - delta[u]) * SCALE) for u in units]
    probs = [probs[u].astype(jnp.bfloat16) for u in units]
    dscores = [dscores[u].astype(jnp.bfloat16) for u in units]
    if far:
        shared = []
        for which, values in ((0, probs), (1, dscores)):
            top = which * (far + window)
            for u in units:
                span = pl.ds(u * lanes, lanes)
                pack_ref[top : top + far, span] = folded(values[u] * far_ref[...], far)
                pack_ref[top + far : top + far + window, span] = folded(values[u] * recent_ref[...], window)
                shared.append(folded(values[u] * older_ref[...], window))
        shared = dot(jnp.concatenate(shared, axis=0), pairing_ref[...], NN_DIMS).astype(jnp.bfloat16)
        for n in range(2 * KEY_VALUE_HEADS):
            span = pl.ds(n * lanes // 2, lanes // 2)
            pack_ref[2 * (far + window) :, span] = shared[n * window : (n + 1) * window]
    key_grad = [dot(dscores[u], q[u], NN_DIMS) for u in units]
    value_grad = [dot(probs[u], g[u], NN_DIMS) for u in units]
    for u in units:
        for which, grad in ((0, key_grad[u]), (1, value_grad[u])):
            own_ref[which, :, feats[u]] = grad[rows:]
            leaving = grad[:rows].astype(jnp.bfloat16)
            if passed:
                leaving = jnp.where(lax.axis_index("ctx") == 0, passed[which][:, feats[u]], leaving)
            other_ref[which, :, feats[u]] = leaving
    if not far:
        for u in units:
            out = dot(probs[u], v[u], TN_DIMS)
            attn_ref[:, wide[u]] = spread_heads(out, rows).astype(jnp.bfloat16)
            out = dot(dscores[u], k[u], TN_DIMS)
            gq_ref[:, wide[u]] = spread_heads(out, rows).astype(jnp.bfloat16)


def attention(far, first_slot, slots, q, g, k, v, first_k, first_v, prepared, passed=()):
    rows = q.shape[1]
    lanes = GROUP_RATIO * rows

    def at(array, start):
        return pl.BlockSpec((None, *array.shape[1:]), lambda s: (s + start, 0, 0))

    of_q = at(q, first_slot)
    partial = (slots, 2, *k.shape[1:])
    of_partial = pl.BlockSpec((None, *partial[1:]), lambda s: (s, 0, 0, 0))
    vmem = pl.BlockSpec(memory_space=pltpu.VMEM)
    out_shape = [jax.ShapeDtypeStruct(partial, jnp.float32), jax.ShapeDtypeStruct(partial, jnp.bfloat16)]
    out_specs = [of_partial, of_partial]
    if far:
        coded = (2 * far + 3 * rows // 4, KEY_VALUE_HEADS * lanes)
        out_shape.insert(0, jax.ShapeDtypeStruct(coded, jnp.bfloat16))
        out_specs.insert(0, pl.BlockSpec(coded, lambda s: (0, 0)))
    else:
        out_shape = [pltpu.HBM(q.shape, q.dtype)] * 2 + out_shape
        out_specs = [of_q, of_q] + out_specs
    return pl.pallas_call(
        functools.partial(attention_body, far, first_slot, rows),
        grid=(slots,),
        in_specs=[of_q, of_q, at(k, first_slot), at(v, first_slot), at(*first_k), at(*first_v)] + [vmem] * 3
        + [at(*array) for array in passed],
        out_specs=out_specs,
        out_shape=out_shape,
        compiler_params=PARAMS,
        cost_estimate=CHEAP,
    )(q, g, k, v, first_k[0], first_v[0], *prepared, *[array for array, _ in passed])


def prepare_body(rows, facts_ref, bias_ref, factors_ref, partner_ref, pairing_ref):
    lanes = GROUP_RATIO * rows
    for slot in range(2):
        allowed, *parts = masks(facts_ref, slot, rows, lanes)
        bias_ref[slot] = jnp.where(allowed, 0.0, -1e30)
    for ref, parts in ((factors_ref, parts), (partner_ref, masks(facts_ref, 2, rows, lanes)[1:])):
        for i, part in enumerate(parts):
            ref[i] = as_factor(part)
    pairing_ref[...] = pairing(rows, lanes)


def prepare(rows, facts):
    lanes = GROUP_RATIO * rows
    vmem = pl.BlockSpec(memory_space=pltpu.VMEM)
    return pl.pallas_call(
        functools.partial(prepare_body, rows),
        in_specs=[pl.BlockSpec(memory_space=pltpu.SMEM)],
        out_specs=[vmem] * 4,
        out_shape=[
            jax.ShapeDtypeStruct((2, 2 * rows, lanes), jnp.float32),
            jax.ShapeDtypeStruct((3, 2 * rows, lanes), jnp.bfloat16),
            jax.ShapeDtypeStruct((3, 2 * rows, lanes), jnp.bfloat16),
            jax.ShapeDtypeStruct((lanes, lanes // 2), jnp.bfloat16),
        ],
        compiler_params=PARAMS,
        cost_estimate=CHEAP,
    )(facts)


def rebuild_body(
    far, rows, pack_ref, near_ref, first_ref, zero_ref, factors_ref, pairing_ref, _a, _b, attn_ref, gq_ref, gk_ref, gv_ref
):
    lanes = GROUP_RATIO * rows
    window = rows // 4
    recent, older, query = (factors_ref[i] for i in range(3))
    for which, out_ref in ((0, gk_ref), (1, gv_ref)):
        arrived = jnp.where(lax.axis_index("ctx") == 0, first_ref[which].astype(jnp.float32), 0.0)
        out_ref[...] = (zero_ref[which] + arrived).astype(jnp.bfloat16)
    shared = [
        pack_ref[2 * (far + window) :, pl.ds(n * lanes // 2, lanes // 2)]
        for n in range(2 * KEY_VALUE_HEADS)
    ]
    shared = dot(jnp.concatenate(shared, axis=0), pairing_ref[...], NT_DIMS).astype(jnp.bfloat16)

    def spread(part):
        return jnp.concatenate([part] * (2 * rows // part.shape[0]), axis=0)

    for which, side_index, out_ref in ((0, 1, attn_ref), (1, 0, gq_ref)):
        top = which * (far + window)
        for u in range(KEY_VALUE_HEADS):
            feats = pl.ds(u * HEAD_SIZE, HEAD_SIZE)
            wide = pl.ds(u * GROUP_RATIO * HEAD_SIZE, GROUP_RATIO * HEAD_SIZE)
            span = pl.ds(u * lanes, lanes)
            side = jnp.concatenate([first_ref[side_index, :, feats], near_ref[side_index, :, feats]], axis=0)
            n = which * KEY_VALUE_HEADS + u
            value = spread(pack_ref[top : top + far, span]) * query
            value += spread(pack_ref[top + far : top + far + window, span]) * recent
            value += spread(shared[n * window : (n + 1) * window]) * older
            out_ref[:, wide] = spread_heads(dot(value, side, TN_DIMS), rows).astype(jnp.bfloat16)


def rebuild(far, pack, kv_near, arrived, own_zero, factors, pairs, attn, gq):
    rows = attn.shape[1]

    def at(array, slot):
        return pl.BlockSpec((None, *array.shape[1:]), lambda i: (slot, 0, 0))

    anywhere = pl.BlockSpec(memory_space=pl.ANY)
    return pl.pallas_call(
        functools.partial(rebuild_body, far, rows),
        grid=(1,),
        in_specs=[pl.BlockSpec(memory_space=pltpu.VMEM)] * 6 + [anywhere, anywhere],
        out_specs=[at(attn, 1), at(gq, 1), at(kv_near, 0), at(kv_near, 0)],
        out_shape=[pltpu.HBM(attn.shape, attn.dtype)] * 2 + [pltpu.HBM(kv_near.shape, kv_near.dtype)] * 2,
        input_output_aliases={6: 0, 7: 1},
        compiler_params=PARAMS,
        cost_estimate=LONG,
    )(pack, kv_near, arrived, own_zero, factors, pairs, attn, gq)


def cut_body(
    flags_in, lengths_in, tiles_in, k_ref, v_ref,
    form_ref, facts_ref, second_ref,
    flags_ref, lengths_ref, tiles_ref, scalar_sems, sems,
):
    scalars = ((flags_in, flags_ref), (lengths_in, lengths_ref), (tiles_in, tiles_ref))
    scalars = [pltpu.make_async_copy(a, b, scalar_sems.at[i]) for i, (a, b) in enumerate(scalars)]
    copies = [
        pltpu.make_async_copy(ref.at[1], second_ref.at[i], sems.at[i])
        for i, ref in enumerate((k_ref, v_ref))
    ]
    for copy in scalars + copies:
        copy.start()
    for copy in scalars:
        copy.wait()
    rank = lax.axis_index("dp")
    ctx = lax.axis_index("ctx")
    partner = jnp.bitwise_xor(rank, lax.axis_size("dp") // 2)
    longest = jnp.maximum(lengths_ref[0, 2 * rank + 1], lengths_ref[0, 2 * partner + 1])
    form_ref[0] = flags_ref[rank] * jnp.where(longest > k_ref.shape[1] // 4, 2, 1)
    for which, seq in enumerate((2 * rank, 2 * rank + 1, 2 * partner + 1)):
        end = jnp.int32(0)
        for d in range(NDOC - 1):
            end = end + lengths_ref[d, seq]
            facts_ref[which * NDOC + d] = end
        facts_ref[which * NDOC + NDOC - 1] = tiles_ref[ctx, 0, seq]
    for copy in copies:
        copy.wait()


def cut(flags, lengths, tiles, k, v):
    smem = pl.BlockSpec(memory_space=pltpu.SMEM)
    vmem = pl.BlockSpec(memory_space=pltpu.VMEM)
    anywhere = pl.BlockSpec(memory_space=pl.ANY)
    whole = jax.ShapeDtypeStruct(k.shape, k.dtype)
    return pl.pallas_call(
        cut_body,
        in_specs=[anywhere] * 5,
        out_specs=[smem, smem, vmem],
        out_shape=[
            jax.ShapeDtypeStruct((1,), jnp.int32),
            jax.ShapeDtypeStruct((3 * NDOC,), jnp.int32),
            whole,
        ],
        scratch_shapes=[pltpu.SMEM(x.shape, x.dtype) for x in (flags, lengths, tiles)]
        + [pltpu.SemaphoreType.DMA((3,)), pltpu.SemaphoreType.DMA((2,))],
        cost_estimate=CHEAP,
    )(flags, lengths, tiles, k, v)


def finish_body(partner_ref, _a, _b, gk_ref, gv_ref):
    gk_ref[...] = partner_ref[0]
    gv_ref[...] = partner_ref[1]


def finish(grads_partner, gk, gv):
    anywhere = pl.BlockSpec(memory_space=pl.ANY)
    second = pl.BlockSpec((None, *gk.shape[1:]), lambda i: (1, 0, 0))
    return pl.pallas_call(
        finish_body,
        grid=(1,),
        in_specs=[pl.BlockSpec(gk.shape, lambda i: (0, 0, 0)), anywhere, anywhere],
        out_specs=[second, second],
        out_shape=[pltpu.HBM(gk.shape, gk.dtype)] * 2,
        input_output_aliases={1: 0, 2: 1},
        compiler_params=PARAMS,
        cost_estimate=CHEAP,
    )(grads_partner, gk, gv)


def to_next(value):
    return lax.ppermute(value, "ctx", [(0, 1)])


def to_owner(value):
    return lax.ppermute(value, "ctx", [(1, 0)])


def swapped(value):
    return lax.ppermute(value, "ctx", [(0, 1), (1, 0)])


def to_partner(value):
    size = lax.axis_size("dp")
    return lax.ppermute(value, "dp", [(s, s ^ (size // 2)) for s in range(size)])


def joined(own, arrived):
    return (own + arrived.astype(jnp.float32)).astype(jnp.bfloat16)


def stay(q, k, v, g, facts, second):
    bias, factors, _, pairs = prepare(q.shape[1], facts)
    first_k = swapped(k)
    v_later, first_k = lax.optimization_barrier((v, first_k))
    first_v = swapped(v_later)
    attn, gq, own, leaving = attention(
        0, 0, 2, q, g, k, v, (first_k, 0), (first_v, 0), (bias, factors, pairs)
    )
    arrived = swapped(leaving)
    grads = joined(own, jnp.where(lax.axis_index("ctx") == 0, arrived, 0))
    return attn, gq, grads[:, 0], grads[:, 1]


def trade(far, q, k, v, g, facts, second):
    bias, factors, partner_factors, pairs = prepare(q.shape[1], facts)
    arrived = swapped(second)
    kv_partner = to_partner(second)
    pack, own_second, leaving = attention(
        far, 1, 1, q, g, k, v, (arrived, 0), (arrived, 1), (bias, factors, pairs), [(k, 0), (v, 0)]
    )
    arrived = swapped(leaving[0])
    pack_partner = to_partner(pack)
    grads = joined(own_second[0], jnp.where(lax.axis_index("ctx") == 0, arrived, 0))
    grads_partner = to_partner(grads)
    attn, gq, own_zero, leaving = attention(
        0, 0, 1, q, g, k, v, (arrived, 0), (arrived, 1), (bias, factors, pairs), [(kv_partner, 0), (kv_partner, 1)]
    )
    arrived = swapped(leaving[0])
    attn, gq, gk, gv = rebuild(
        far, pack_partner, kv_partner, arrived, own_zero[0], partner_factors, pairs, attn, gq
    )
    return attn, gq, *finish(grads_partner, gk, gv)


def two_rank_shards(query_proj, key_proj, value_proj, grad_attn, doc_lengths, mask_tiles, pair_flags):
    rows = query_proj.shape[1]
    form, *cuts = cut(
        pair_flags, doc_lengths.T, mask_tiles.transpose(1, 2, 0), key_proj, value_proj
    )
    forms = (stay, functools.partial(trade, rows // 4), functools.partial(trade, rows // 2))
    return lax.switch(form[0], forms, query_proj, key_proj, value_proj, grad_attn, *cuts)


def from_partner(value, axis, distance):
    mask = 2**distance
    pairs = [(source, source ^ mask) for source in range(lax.axis_size(axis))]
    return lax.ppermute(value, axis, pairs)


def sequence_core(
    query_rows, sequence_keys, sequence_values, sequence_gradients, lengths, tile_table, row_start
):
    rows = query_rows.shape[0]
    length_total = sequence_keys.shape[0]
    groups = sequence_keys.shape[1] // HEAD_SIZE
    group_ratio = QUERY_HEADS // KEY_VALUE_HEADS
    scale = HEAD_SIZE ** (-0.5)
    row_pos = row_start + jnp.arange(rows, dtype=jnp.int32)
    col_pos = jnp.arange(length_total, dtype=jnp.int32)
    ends = jnp.cumsum(lengths)[:-1]
    row_doc = jnp.sum((row_pos[:, None] >= ends[None, :]).astype(jnp.int32), axis=1)
    col_doc = jnp.sum((col_pos[:, None] >= ends[None, :]).astype(jnp.int32), axis=1)
    tile_count = tile_table.shape[0]
    tile_len = length_total // tile_count
    tile_ids = jnp.arange(tile_count, dtype=jnp.int32)
    row_pick = ((row_pos // tile_len)[:, None] == tile_ids[None, :]).astype(jnp.float32)
    col_pick = ((col_pos // tile_len)[:, None] == tile_ids[None, :]).astype(jnp.float32)
    tile_map = jnp.dot(jnp.dot(row_pick, tile_table.astype(jnp.float32)), col_pick.T) > 0.5
    allowed = (
        (col_pos[None, :] <= row_pos[:, None])
        & ((col_doc[None, :] == row_doc[:, None]) | (col_doc[None, :] == 0))
        & tile_map
    )
    heads_of_queries = query_rows.reshape(rows, groups, group_ratio, HEAD_SIZE)
    heads_of_keys = sequence_keys.reshape(length_total, groups, HEAD_SIZE)
    heads_of_values = sequence_values.reshape(length_total, groups, HEAD_SIZE)
    head_gradients = sequence_gradients.reshape(rows, groups, group_ratio, HEAD_SIZE)
    scores = (
        jnp.einsum(
            "igrd,jgd->grij", heads_of_queries, heads_of_keys, preferred_element_type=jnp.float32
        )
        * scale
    )
    scores = jnp.where(allowed, scores, -1e30)
    peak = jnp.max(scores, axis=-1, keepdims=True)
    expd = jnp.where(allowed, jnp.exp(scores - peak), 0.0)
    probs = expd / jnp.sum(expd, axis=-1, keepdims=True)
    probs_b = probs.astype(jnp.bfloat16)
    attn = jnp.einsum(
        "grij,jgd->igrd", probs_b, heads_of_values, preferred_element_type=jnp.float32
    ).astype(jnp.bfloat16)
    delta = jnp.transpose(
        jnp.sum(head_gradients.astype(jnp.float32) * attn.astype(jnp.float32), axis=-1), (1, 2, 0)
    )
    value_gradient = jnp.einsum(
        "grij,igrd->jgd", probs_b, head_gradients, preferred_element_type=jnp.float32
    )
    dprobs = jnp.einsum(
        "igrd,jgd->grij", head_gradients, heads_of_values, preferred_element_type=jnp.float32
    )
    dscores = (probs * (dprobs - delta[..., None]) * scale).astype(jnp.bfloat16)
    grad_q = jnp.einsum(
        "grij,jgd->igrd", dscores, heads_of_keys, preferred_element_type=jnp.float32
    )
    key_gradient = jnp.einsum(
        "grij,igrd->jgd", dscores, heads_of_queries, preferred_element_type=jnp.float32
    )
    return (
        attn.reshape(rows, -1),
        grad_q.astype(jnp.bfloat16).reshape(rows, -1),
        key_gradient.reshape(length_total, -1),
        value_gradient.reshape(length_total, -1),
    )


def attend(query_rows, keys_in, values_in, grads_in, lengths_all, tiles_all, first_id, second_id):
    seq_ids = jnp.stack([first_id, second_id])
    lengths_pair = jnp.take(lengths_all, seq_ids, axis=0)
    tiles_pair = jnp.take(tiles_all, seq_ids, axis=0)
    ctx_rank = lax.axis_index("ctx")
    seq_dev = query_rows.shape[1]
    keys_all, values_all = (
        lax.all_gather(keys_in, "ctx", axis=1, tiled=True),
        lax.all_gather(values_in, "ctx", axis=1, tiled=True),
    )
    pieces = [
        sequence_core(
            query_rows[seq_slot],
            keys_all[seq_slot],
            values_all[seq_slot],
            grads_in[seq_slot],
            lengths_pair[seq_slot],
            tiles_pair[seq_slot],
            ctx_rank * seq_dev,
        )
        for seq_slot in range(2)
    ]
    attn = jnp.stack([pieces[0][0], pieces[1][0]])
    grad_q = jnp.stack([pieces[0][1], pieces[1][1]])
    key_terms = jnp.stack([pieces[0][2], pieces[1][2]])
    value_terms = jnp.stack([pieces[0][3], pieces[1][3]])
    key_sums, value_sums = (
        lax.psum_scatter(key_terms, "ctx", scatter_dimension=1, tiled=True),
        lax.psum_scatter(value_terms, "ctx", scatter_dimension=1, tiled=True),
    )
    return (attn, grad_q, key_sums.astype(jnp.bfloat16), value_sums.astype(jnp.bfloat16))


def take_second(mine, arrived, swapped):
    return jnp.stack([mine[0], jnp.where(swapped, arrived, mine[1])])


def shards(query_proj, key_proj, value_proj, grad_attn, doc_lengths, mask_tiles, pair_flags):
    dp_size = lax.axis_size("dp")
    dp_rank = lax.axis_index("dp")
    far_bit = dp_size.bit_length() - 2
    partner = jnp.bitwise_xor(dp_rank, dp_size // 2)
    pair_flag = lax.dynamic_index_in_dim(pair_flags, dp_rank, 0, keepdims=False)
    swapped = pair_flag == 1
    first_id = 2 * dp_rank
    second_id = jnp.where(swapped, 2 * partner + 1, 2 * dp_rank + 1)
    arrived = from_partner((query_proj[1], key_proj[1], value_proj[1], grad_attn[1]), "dp", far_bit)
    query_now = take_second(query_proj, arrived[0], swapped)
    key_now = take_second(key_proj, arrived[1], swapped)
    value_now = take_second(value_proj, arrived[2], swapped)
    grad_now = take_second(grad_attn, arrived[3], swapped)
    return attend(
        query_now, key_now, value_now, grad_now, doc_lengths, mask_tiles, first_id, second_id
    )


def solution(mesh):
    in_specs = (
        P("dp", "ctx", None),
        P("dp", "ctx", None),
        P("dp", "ctx", None),
        P("dp", "ctx", None),
        P(),
        P(),
        P(),
    )
    out_specs = (
        P("dp", "ctx", None),
        P("dp", "ctx", None),
        P("dp", "ctx", None),
        P("dp", "ctx", None),
    )
    form = two_rank_shards if mesh.shape["ctx"] == 2 else shards
    return jax.shard_map(form, mesh=mesh, in_specs=in_specs, out_specs=out_specs, check_vma=False)
```

```python
import functools

import jax
import jax.numpy as jnp
from jax import lax
from jax.experimental import pallas as pl
from jax.experimental.pallas import tpu as pltpu
from jax.sharding import PartitionSpec as P

QUERY_HEADS = 32
KEY_VALUE_HEADS = 8
HEAD_SIZE = 128
GROUP_RATIO = QUERY_HEADS // KEY_VALUE_HEADS
SCALE = HEAD_SIZE ** (-0.5)
LOG2_E = 1.4426950408889634
WIDE = GROUP_RATIO * HEAD_SIZE
NDOC = 8
PARAMS = pltpu.CompilerParams(vmem_limit_bytes=32 * 2**20)
LONG = pl.CostEstimate(flops=1, bytes_accessed=2**27, transcendentals=0)
CHEAP = pl.CostEstimate(flops=1, bytes_accessed=1, transcendentals=0)
NT_DIMS = (((1,), (1,)), ((), ()))
TN_DIMS = (((0,), (0,)), ((), ()))
NN_DIMS = (((1,), (0,)), ((), ()))


def dot(a, b, dims):
    return lax.dot_general(a, b, dims, preferred_element_type=jnp.float32)


def masks(facts_ref, which, rows, lanes):
    ctx = lax.axis_index("ctx")
    key_index = lax.broadcasted_iota(jnp.int32, (2 * rows, 1), 0)
    col_pos = key_index + (ctx - 1) * rows
    row_pos = lax.rem(lax.broadcasted_iota(jnp.int32, (1, lanes), 1), rows) + ctx * rows
    col_doc = jnp.zeros_like(col_pos)
    row_doc = jnp.zeros_like(row_pos)
    for d in range(NDOC - 1):
        end = facts_ref[which * NDOC + d]
        col_doc = col_doc + (col_pos >= end).astype(jnp.int32)
        row_doc = row_doc + (row_pos >= end).astype(jnp.int32)
    seen = (key_index >= rows) | (facts_ref[which * NDOC + NDOC - 1] == 1)
    col_doc = jnp.where(seen & (col_pos >= 0), col_doc, -1)
    back = row_pos - col_pos
    own = (col_doc == row_doc) & (back >= 0)
    query = (col_doc == 0) & (row_doc != 0)
    return own | query, own & (back < rows // 4), own & (back >= rows // 4), query


def as_factor(mask):
    return jnp.where(mask, 1.0, 0.0).astype(jnp.bfloat16)


def pairing(rows, lanes):
    window = rows // 4
    lane = lax.broadcasted_iota(jnp.int32, (lanes, lanes // 2), 0)
    shared = lax.broadcasted_iota(jnp.int32, (lanes, lanes // 2), 1)
    target = lane // (2 * window) * window + lax.rem(lane, window)
    return as_factor(target == shared)


def stacked_heads(block, rows):
    return jnp.concatenate(
        [block[:, h * HEAD_SIZE : (h + 1) * HEAD_SIZE] for h in range(GROUP_RATIO)], axis=0
    )


def spread_heads(value, rows):
    return jnp.concatenate([value[h * rows : (h + 1) * rows] for h in range(GROUP_RATIO)], axis=1)


def folded(value, bound):
    total = value[:bound]
    for b in range(1, value.shape[0] // bound):
        total = total + value[b * bound : (b + 1) * bound]
    return total


def total(own, arrived):
    arrived = jnp.where(lax.axis_index("ctx") == 0, arrived.astype(jnp.float32), 0.0)
    return (own + arrived).astype(jnp.bfloat16)


def scores_body(
    far, slot, first, passed, rows,
    q_ref, g_ref, k_ref, v_ref, first_k_ref, first_v_ref, passed_k_ref, passed_v_ref, bias_ref, *rest
):
    lanes = GROUP_RATIO * rows
    window = rows // 4
    if far:
        factors_ref, pairing_ref, out_hbm, own_ref, leaving_ref, out_ref, shared_ref, sem = rest
        recent_ref, older_ref, far_ref = (factors_ref.at[i] for i in range(3))
        store = pltpu.make_async_copy(out_ref, out_hbm, sem)
    elif len(rest) > 3:
        before_ref, out_ref, own_ref, leaving_ref, grads_ref = rest
        for which, ref in ((0, first_k_ref), (1, first_v_ref)):
            grads_ref[which] = total(before_ref[which], ref[first[which]])
    else:
        out_ref, own_ref, leaving_ref = rest
    sends = lax.axis_index("ctx") == 0

    def middle(scores, dprobs):
        scores = scores * (SCALE * LOG2_E) + bias_ref[slot]
        expd = jnp.exp2(scores - jnp.max(scores, axis=0, keepdims=True))
        inverse = 1.0 / jnp.sum(expd, axis=0, keepdims=True)
        delta = jnp.sum(expd * dprobs, axis=0, keepdims=True) * inverse
        probs = (expd * inverse).astype(jnp.bfloat16)
        return probs, (expd * (inverse * SCALE) * (dprobs - delta)).astype(jnp.bfloat16)

    units = range(KEY_VALUE_HEADS)
    feats = [pl.ds(u * HEAD_SIZE, HEAD_SIZE) for u in units]
    wide = [pl.ds(u * WIDE, WIDE) for u in units]
    q = [stacked_heads(q_ref[slot, :, w], rows) for w in wide]
    g = [stacked_heads(g_ref[slot, :, w], rows) for w in wide]
    k = [jnp.concatenate([first_k_ref[first[0], :, f], k_ref[slot, :, f]], axis=0) for f in feats]
    v = [jnp.concatenate([first_v_ref[first[1], :, f], v_ref[slot, :, f]], axis=0) for f in feats]
    scores = [dot(a, b, NT_DIMS) for a, b in zip(k, q)]
    dprobs = [dot(a, b, NT_DIMS) for a, b in zip(v, g)]
    pairs = [middle(a, b) for a, b in zip(scores, dprobs)]
    for n, u in enumerate(units):
        for which, value in enumerate(pairs[n]):
            if not far:
                out_ref[which, u] = value
                continue
            span = pl.ds(u * lanes, lanes)
            top = which * (far + window)
            out_ref[top : top + far, span] = folded(value * far_ref[...], far)
            out_ref[top + far : top + far + window, span] = folded(value * recent_ref[...], window)
            place = (which * KEY_VALUE_HEADS + u) * window
            shared_ref[pl.ds(place, window)] = folded(value * older_ref[...], window)
    if far:
        shared = dot(shared_ref[...], pairing_ref[...], NN_DIMS).astype(jnp.bfloat16)
        for n in range(2 * KEY_VALUE_HEADS):
            span = pl.ds(n * lanes // 2, lanes // 2)
            out_ref[2 * (far + window) :, span] = shared[n * window : (n + 1) * window]
        store.start()
    for which, sides in ((0, q), (1, g)):
        passed_ref = (passed_k_ref, passed_v_ref)[which]
        for n, f in enumerate(feats):
            grad = dot(pairs[n][1 - which], sides[n], NN_DIMS)
            own_ref[which, :, f] = grad[rows:]
            leaving_ref[which, :, f] = jnp.where(
                sends, passed_ref[passed[which], :, f], grad[:rows].astype(jnp.bfloat16)
            )
    if far:
        store.wait()


def scores(far, slot, q, g, k, v, first, passed, bias, *more):
    rows = q.shape[1]
    lanes = GROUP_RATIO * rows
    vmem = pl.BlockSpec(memory_space=pltpu.VMEM)
    anywhere = pl.BlockSpec(memory_space=pl.ANY)
    partial = (2, *k.shape[1:])
    leaving = jax.ShapeDtypeStruct(partial, jnp.bfloat16)
    scratch = []
    if far:
        coded = (2 * far + 3 * rows // 4, KEY_VALUE_HEADS * lanes)
        out_specs = [anywhere, vmem, vmem]
        out_shape = [pltpu.HBM(coded, jnp.bfloat16), jax.ShapeDtypeStruct(partial, jnp.float32), leaving]
        scratch = [
            pltpu.VMEM(coded, jnp.bfloat16),
            pltpu.VMEM((2 * KEY_VALUE_HEADS * rows // 4, lanes), jnp.bfloat16),
            pltpu.SemaphoreType.DMA,
        ]
    else:
        coded = (2, KEY_VALUE_HEADS, 2 * rows, lanes)
        out_specs = [vmem] * (3 + len(more))
        out_shape = [
            jax.ShapeDtypeStruct(coded, jnp.bfloat16),
            jax.ShapeDtypeStruct(partial, jnp.float32),
            leaving,
        ] + [leaving for _ in more]
    return pl.pallas_call(
        functools.partial(
            scores_body, far, slot, (first[0][1], first[1][1]), (passed[0][1], passed[1][1]), rows
        ),
        in_specs=[vmem] * (9 + len(more)),
        out_specs=out_specs,
        out_shape=out_shape,
        scratch_shapes=scratch,
        compiler_params=PARAMS,
        cost_estimate=CHEAP,
    )(q, g, k, v, first[0][0], first[1][0], passed[0][0], passed[1][0], bias, *more)


def prepare_body(
    rows, facts_ref, q_in, g_in, k_in, v_in,
    bias_ref, factors_ref, partner_ref, pairing_ref, q_ref, g_ref, k_ref, v_ref, sems,
):
    loads = ((q_in, q_ref), (g_in, g_ref), (k_in, k_ref), (v_in, v_ref))
    loads = [pltpu.make_async_copy(a, b, sems.at[i]) for i, (a, b) in enumerate(loads)]
    for load in loads:
        load.start()
    lanes = GROUP_RATIO * rows
    for slot in range(2):
        allowed, *parts = masks(facts_ref, slot, rows, lanes)
        bias_ref[slot] = jnp.where(allowed, 0.0, -1e30)
    for ref, parts in ((factors_ref, parts), (partner_ref, masks(facts_ref, 2, rows, lanes)[1:])):
        for i, part in enumerate(parts):
            ref[i] = as_factor(part)
    pairing_ref[...] = pairing(rows, lanes)
    for load in loads:
        load.wait()


def prepare(facts, q, g, k, v):
    rows = q.shape[1]
    lanes = GROUP_RATIO * rows
    vmem = pl.BlockSpec(memory_space=pltpu.VMEM)
    anywhere = pl.BlockSpec(memory_space=pl.ANY)
    return pl.pallas_call(
        functools.partial(prepare_body, rows),
        in_specs=[pl.BlockSpec(memory_space=pltpu.SMEM)] + [anywhere] * 4,
        out_specs=[vmem] * 8,
        out_shape=[
            jax.ShapeDtypeStruct((2, 2 * rows, lanes), jnp.float32),
            jax.ShapeDtypeStruct((3, 2 * rows, lanes), jnp.bfloat16),
            jax.ShapeDtypeStruct((3, 2 * rows, lanes), jnp.bfloat16),
            jax.ShapeDtypeStruct((lanes, lanes // 2), jnp.bfloat16),
        ]
        + [jax.ShapeDtypeStruct(x.shape, x.dtype) for x in (q, g, k, v)],
        scratch_shapes=[pltpu.SemaphoreType.DMA((4,))],
        compiler_params=PARAMS,
        cost_estimate=CHEAP,
    )(facts, q, g, k, v)


def outputs_body(slot, first, rows, coded_ref, k_ref, v_ref, first_k_ref, first_v_ref, *rest):
    attn_ref, gq_ref = rest[-2:]
    for u in range(KEY_VALUE_HEADS):
        feats = pl.ds(u * HEAD_SIZE, HEAD_SIZE)
        wide = pl.ds(u * GROUP_RATIO * HEAD_SIZE, GROUP_RATIO * HEAD_SIZE)
        v = jnp.concatenate([first_v_ref[first[1], :, feats], v_ref[slot, :, feats]], axis=0)
        attn_ref[:, wide] = spread_heads(dot(coded_ref[0, u], v, TN_DIMS), rows).astype(jnp.bfloat16)
        k = jnp.concatenate([first_k_ref[first[0], :, feats], k_ref[slot, :, feats]], axis=0)
        gq_ref[:, wide] = spread_heads(dot(coded_ref[1, u], k, TN_DIMS), rows).astype(jnp.bfloat16)


def outputs(slot, coded, k, v, first, shape, earlier=()):
    vmem = pl.BlockSpec(memory_space=pltpu.VMEM)
    of_q = pl.BlockSpec((None, *shape[1:]), lambda i: (slot, 0, 0))
    return pl.pallas_call(
        functools.partial(outputs_body, slot, (first[0][1], first[1][1]), shape[1]),
        grid=(1,),
        in_specs=[vmem] * 5 + [pl.BlockSpec(memory_space=pl.ANY) for _ in earlier],
        out_specs=[of_q, of_q],
        out_shape=[pltpu.HBM(shape, jnp.bfloat16)] * 2,
        input_output_aliases={5: 0, 6: 1} if earlier else {},
        compiler_params=PARAMS,
        cost_estimate=CHEAP,
    )(coded, k, v, first[0][0], first[1][0], *earlier)


def rebuild_body(
    far, rows, pack_ref, near_ref, first_ref, zero_ref, factors_ref, pairing_ref, _a, _b, attn_ref, gq_ref, gk_ref, gv_ref
):
    lanes = GROUP_RATIO * rows
    window = rows // 4
    recent, older, query = (factors_ref[i] for i in range(3))
    for which, out_ref in ((0, gk_ref), (1, gv_ref)):
        out_ref[...] = total(zero_ref[which], first_ref[which])
    shared = [
        pack_ref[2 * (far + window) :, pl.ds(n * lanes // 2, lanes // 2)]
        for n in range(2 * KEY_VALUE_HEADS)
    ]
    shared = dot(jnp.concatenate(shared, axis=0), pairing_ref[...], NT_DIMS).astype(jnp.bfloat16)

    def spread(part):
        return jnp.concatenate([part] * (2 * rows // part.shape[0]), axis=0)

    for which, side_index, out_ref in ((0, 1, attn_ref), (1, 0, gq_ref)):
        top = which * (far + window)
        for u in range(KEY_VALUE_HEADS):
            feats = pl.ds(u * HEAD_SIZE, HEAD_SIZE)
            wide = pl.ds(u * GROUP_RATIO * HEAD_SIZE, GROUP_RATIO * HEAD_SIZE)
            span = pl.ds(u * lanes, lanes)
            side = jnp.concatenate([first_ref[side_index, :, feats], near_ref[side_index, :, feats]], axis=0)
            n = which * KEY_VALUE_HEADS + u
            value = spread(pack_ref[top : top + far, span]) * query
            value += spread(pack_ref[top + far : top + far + window, span]) * recent
            value += spread(shared[n * window : (n + 1) * window]) * older
            out_ref[:, wide] = spread_heads(dot(value, side, TN_DIMS), rows).astype(jnp.bfloat16)


def rebuild(far, pack, kv_near, arrived, own_zero, factors, pairs, attn, gq):
    rows = attn.shape[1]

    def at(array, slot):
        return pl.BlockSpec((None, *array.shape[1:]), lambda i: (slot, 0, 0))

    anywhere = pl.BlockSpec(memory_space=pl.ANY)
    return pl.pallas_call(
        functools.partial(rebuild_body, far, rows),
        grid=(1,),
        in_specs=[pl.BlockSpec(memory_space=pltpu.VMEM)] * 6 + [anywhere, anywhere],
        out_specs=[at(attn, 1), at(gq, 1), at(kv_near, 0), at(kv_near, 0)],
        out_shape=[pltpu.HBM(attn.shape, attn.dtype)] * 2 + [pltpu.HBM(kv_near.shape, kv_near.dtype)] * 2,
        input_output_aliases={6: 0, 7: 1},
        compiler_params=PARAMS,
        cost_estimate=LONG,
    )(pack, kv_near, arrived, own_zero, factors, pairs, attn, gq)


def cut_body(
    flags_in, lengths_in, tiles_in, k_ref, v_ref,
    form_ref, facts_ref, second_ref,
    flags_ref, lengths_ref, tiles_ref, scalar_sems, sems,
):
    scalars = ((flags_in, flags_ref), (lengths_in, lengths_ref), (tiles_in, tiles_ref))
    scalars = [pltpu.make_async_copy(a, b, scalar_sems.at[i]) for i, (a, b) in enumerate(scalars)]
    copies = [
        pltpu.make_async_copy(ref.at[1], second_ref.at[i], sems.at[i])
        for i, ref in enumerate((k_ref, v_ref))
    ]
    for copy in scalars + copies:
        copy.start()
    for copy in scalars:
        copy.wait()
    rank = lax.axis_index("dp")
    ctx = lax.axis_index("ctx")
    partner = jnp.bitwise_xor(rank, lax.axis_size("dp") // 2)
    longest = jnp.maximum(lengths_ref[0, 2 * rank + 1], lengths_ref[0, 2 * partner + 1])
    form_ref[0] = flags_ref[rank] * jnp.where(longest > k_ref.shape[1] // 4, 2, 1)
    for which, seq in enumerate((2 * rank, 2 * rank + 1, 2 * partner + 1)):
        end = jnp.int32(0)
        for d in range(NDOC - 1):
            end = end + lengths_ref[d, seq]
            facts_ref[which * NDOC + d] = end
        facts_ref[which * NDOC + NDOC - 1] = tiles_ref[ctx, 0, seq]
    for copy in copies:
        copy.wait()


def cut(flags, lengths, tiles, k, v):
    smem = pl.BlockSpec(memory_space=pltpu.SMEM)
    vmem = pl.BlockSpec(memory_space=pltpu.VMEM)
    anywhere = pl.BlockSpec(memory_space=pl.ANY)
    whole = jax.ShapeDtypeStruct(k.shape, k.dtype)
    return pl.pallas_call(
        cut_body,
        in_specs=[anywhere] * 5,
        out_specs=[smem, smem, vmem],
        out_shape=[
            jax.ShapeDtypeStruct((1,), jnp.int32),
            jax.ShapeDtypeStruct((3 * NDOC,), jnp.int32),
            whole,
        ],
        scratch_shapes=[pltpu.SMEM(x.shape, x.dtype) for x in (flags, lengths, tiles)]
        + [pltpu.SemaphoreType.DMA((3,)), pltpu.SemaphoreType.DMA((2,))],
        cost_estimate=CHEAP,
    )(flags, lengths, tiles, k, v)


def finish_body(partner_ref, _a, _b, gk_ref, gv_ref):
    gk_ref[...] = partner_ref[0]
    gv_ref[...] = partner_ref[1]


def finish(grads_partner, gk, gv):
    anywhere = pl.BlockSpec(memory_space=pl.ANY)
    second = pl.BlockSpec((None, *gk.shape[1:]), lambda i: (1, 0, 0))
    return pl.pallas_call(
        finish_body,
        grid=(1,),
        in_specs=[pl.BlockSpec(gk.shape, lambda i: (0, 0, 0)), anywhere, anywhere],
        out_specs=[second, second],
        out_shape=[pltpu.HBM(gk.shape, gk.dtype)] * 2,
        input_output_aliases={1: 0, 2: 1},
        compiler_params=PARAMS,
        cost_estimate=CHEAP,
    )(grads_partner, gk, gv)


def to_next(value):
    return lax.ppermute(value, "ctx", [(0, 1)])


def to_owner(value):
    return lax.ppermute(value, "ctx", [(1, 0)])


def swapped(value):
    return lax.ppermute(value, "ctx", [(0, 1), (1, 0)])


def to_partner(value):
    size = lax.axis_size("dp")
    return lax.ppermute(value, "dp", [(s, s ^ (size // 2)) for s in range(size)])


def stay(q, k, v, g, facts, second):
    bias, _, _, _, q, g, k, v = prepare(facts, q, g, k, v)
    arrived = swapped(second)
    first = ((arrived, 0), (arrived, 1))
    coded, own, leaving = scores(0, 1, q, g, k, v, first, ((k, 0), (v, 0)), bias)
    arrived = swapped(leaving)
    done = outputs(1, coded, k, v, first, q.shape)
    first = ((arrived, 0), (arrived, 1))
    coded, own, leaving, grads = scores(0, 0, q, g, k, v, first, ((k, 0), (v, 0)), bias, own)
    arrived = swapped(leaving)
    done = outputs(0, coded, k, v, first, q.shape, done)
    zero = total(own, arrived)
    return *done, jnp.stack([zero[0], grads[0]]), jnp.stack([zero[1], grads[1]])


def trade(far, q, k, v, g, facts, second):
    bias, factors, partner_factors, pairs, q, g, k, v = prepare(facts, q, g, k, v)
    arrived = swapped(second)
    kv_partner = to_partner(second)
    pack, own, leaving = scores(
        far, 1, q, g, k, v, ((arrived, 0), (arrived, 1)), ((k, 0), (v, 0)), bias, factors, pairs
    )
    arrived = swapped(leaving)
    pack_partner = to_partner(pack)
    first = ((arrived, 0), (arrived, 1))
    coded, own, leaving, grads = scores(
        0, 0, q, g, k, v, first, ((kv_partner, 0), (kv_partner, 1)), bias, own
    )
    arrived = swapped(leaving)
    grads_partner = to_partner(grads)
    attn, gq = outputs(0, coded, k, v, first, q.shape)
    attn, gq, gk, gv = rebuild(
        far, pack_partner, kv_partner, arrived, own, partner_factors, pairs, attn, gq
    )
    return attn, gq, *finish(grads_partner, gk, gv)


def two_rank_shards(query_proj, key_proj, value_proj, grad_attn, doc_lengths, mask_tiles, pair_flags):
    rows = query_proj.shape[1]
    form, *cuts = cut(
        pair_flags, doc_lengths.T, mask_tiles.transpose(1, 2, 0), key_proj, value_proj
    )
    forms = (stay, functools.partial(trade, rows // 4), functools.partial(trade, rows // 2))
    return lax.switch(form[0], forms, query_proj, key_proj, value_proj, grad_attn, *cuts)


def from_partner(value, axis, distance):
    mask = 2**distance
    pairs = [(source, source ^ mask) for source in range(lax.axis_size(axis))]
    return lax.ppermute(value, axis, pairs)


def sequence_core(
    query_rows, sequence_keys, sequence_values, sequence_gradients, lengths, tile_table, row_start
):
    rows = query_rows.shape[0]
    length_total = sequence_keys.shape[0]
    groups = sequence_keys.shape[1] // HEAD_SIZE
    group_ratio = QUERY_HEADS // KEY_VALUE_HEADS
    scale = HEAD_SIZE ** (-0.5)
    row_pos = row_start + jnp.arange(rows, dtype=jnp.int32)
    col_pos = jnp.arange(length_total, dtype=jnp.int32)
    ends = jnp.cumsum(lengths)[:-1]
    row_doc = jnp.sum((row_pos[:, None] >= ends[None, :]).astype(jnp.int32), axis=1)
    col_doc = jnp.sum((col_pos[:, None] >= ends[None, :]).astype(jnp.int32), axis=1)
    tile_count = tile_table.shape[0]
    tile_len = length_total // tile_count
    tile_ids = jnp.arange(tile_count, dtype=jnp.int32)
    row_pick = ((row_pos // tile_len)[:, None] == tile_ids[None, :]).astype(jnp.float32)
    col_pick = ((col_pos // tile_len)[:, None] == tile_ids[None, :]).astype(jnp.float32)
    tile_map = jnp.dot(jnp.dot(row_pick, tile_table.astype(jnp.float32)), col_pick.T) > 0.5
    allowed = (
        (col_pos[None, :] <= row_pos[:, None])
        & ((col_doc[None, :] == row_doc[:, None]) | (col_doc[None, :] == 0))
        & tile_map
    )
    heads_of_queries = query_rows.reshape(rows, groups, group_ratio, HEAD_SIZE)
    heads_of_keys = sequence_keys.reshape(length_total, groups, HEAD_SIZE)
    heads_of_values = sequence_values.reshape(length_total, groups, HEAD_SIZE)
    head_gradients = sequence_gradients.reshape(rows, groups, group_ratio, HEAD_SIZE)
    scores = (
        jnp.einsum(
            "igrd,jgd->grij", heads_of_queries, heads_of_keys, preferred_element_type=jnp.float32
        )
        * scale
    )
    scores = jnp.where(allowed, scores, -1e30)
    peak = jnp.max(scores, axis=-1, keepdims=True)
    expd = jnp.where(allowed, jnp.exp(scores - peak), 0.0)
    probs = expd / jnp.sum(expd, axis=-1, keepdims=True)
    probs_b = probs.astype(jnp.bfloat16)
    attn = jnp.einsum(
        "grij,jgd->igrd", probs_b, heads_of_values, preferred_element_type=jnp.float32
    ).astype(jnp.bfloat16)
    delta = jnp.transpose(
        jnp.sum(head_gradients.astype(jnp.float32) * attn.astype(jnp.float32), axis=-1), (1, 2, 0)
    )
    value_gradient = jnp.einsum(
        "grij,igrd->jgd", probs_b, head_gradients, preferred_element_type=jnp.float32
    )
    dprobs = jnp.einsum(
        "igrd,jgd->grij", head_gradients, heads_of_values, preferred_element_type=jnp.float32
    )
    dscores = (probs * (dprobs - delta[..., None]) * scale).astype(jnp.bfloat16)
    grad_q = jnp.einsum(
        "grij,jgd->igrd", dscores, heads_of_keys, preferred_element_type=jnp.float32
    )
    key_gradient = jnp.einsum(
        "grij,igrd->jgd", dscores, heads_of_queries, preferred_element_type=jnp.float32
    )
    return (
        attn.reshape(rows, -1),
        grad_q.astype(jnp.bfloat16).reshape(rows, -1),
        key_gradient.reshape(length_total, -1),
        value_gradient.reshape(length_total, -1),
    )


def attend(query_rows, keys_in, values_in, grads_in, lengths_all, tiles_all, first_id, second_id):
    seq_ids = jnp.stack([first_id, second_id])
    lengths_pair = jnp.take(lengths_all, seq_ids, axis=0)
    tiles_pair = jnp.take(tiles_all, seq_ids, axis=0)
    ctx_rank = lax.axis_index("ctx")
    seq_dev = query_rows.shape[1]
    keys_all, values_all = (
        lax.all_gather(keys_in, "ctx", axis=1, tiled=True),
        lax.all_gather(values_in, "ctx", axis=1, tiled=True),
    )
    pieces = [
        sequence_core(
            query_rows[seq_slot],
            keys_all[seq_slot],
            values_all[seq_slot],
            grads_in[seq_slot],
            lengths_pair[seq_slot],
            tiles_pair[seq_slot],
            ctx_rank * seq_dev,
        )
        for seq_slot in range(2)
    ]
    attn = jnp.stack([pieces[0][0], pieces[1][0]])
    grad_q = jnp.stack([pieces[0][1], pieces[1][1]])
    key_terms = jnp.stack([pieces[0][2], pieces[1][2]])
    value_terms = jnp.stack([pieces[0][3], pieces[1][3]])
    key_sums, value_sums = (
        lax.psum_scatter(key_terms, "ctx", scatter_dimension=1, tiled=True),
        lax.psum_scatter(value_terms, "ctx", scatter_dimension=1, tiled=True),
    )
    return (attn, grad_q, key_sums.astype(jnp.bfloat16), value_sums.astype(jnp.bfloat16))


def take_second(mine, arrived, swapped):
    return jnp.stack([mine[0], jnp.where(swapped, arrived, mine[1])])


def shards(query_proj, key_proj, value_proj, grad_attn, doc_lengths, mask_tiles, pair_flags):
    dp_size = lax.axis_size("dp")
    dp_rank = lax.axis_index("dp")
    far_bit = dp_size.bit_length() - 2
    partner = jnp.bitwise_xor(dp_rank, dp_size // 2)
    pair_flag = lax.dynamic_index_in_dim(pair_flags, dp_rank, 0, keepdims=False)
    swapped = pair_flag == 1
    first_id = 2 * dp_rank
    second_id = jnp.where(swapped, 2 * partner + 1, 2 * dp_rank + 1)
    arrived = from_partner((query_proj[1], key_proj[1], value_proj[1], grad_attn[1]), "dp", far_bit)
    query_now = take_second(query_proj, arrived[0], swapped)
    key_now = take_second(key_proj, arrived[1], swapped)
    value_now = take_second(value_proj, arrived[2], swapped)
    grad_now = take_second(grad_attn, arrived[3], swapped)
    return attend(
        query_now, key_now, value_now, grad_now, doc_lengths, mask_tiles, first_id, second_id
    )


def solution(mesh):
    in_specs = (
        P("dp", "ctx", None),
        P("dp", "ctx", None),
        P("dp", "ctx", None),
        P("dp", "ctx", None),
        P(),
        P(),
        P(),
    )
    out_specs = (
        P("dp", "ctx", None),
        P("dp", "ctx", None),
        P("dp", "ctx", None),
        P("dp", "ctx", None),
    )
    form = two_rank_shards if mesh.shape["ctx"] == 2 else shards
    return jax.shard_map(form, mesh=mesh, in_specs=in_specs, out_specs=out_specs, check_vma=False)
```

```python
import functools

import jax
import jax.numpy as jnp
from jax import lax
from jax.experimental import pallas as pl
from jax.experimental.pallas import tpu as pltpu
from jax.sharding import PartitionSpec as P

QUERY_HEADS = 32
KEY_VALUE_HEADS = 8
HEAD_SIZE = 128
GROUP_RATIO = QUERY_HEADS // KEY_VALUE_HEADS
SCALE = HEAD_SIZE ** (-0.5)
LOG2_E = 1.4426950408889634
WIDE = GROUP_RATIO * HEAD_SIZE
NDOC = 8
PARAMS = pltpu.CompilerParams(vmem_limit_bytes=32 * 2**20)
CHEAP = pl.CostEstimate(flops=1, bytes_accessed=1, transcendentals=0)
NT_DIMS = (((1,), (1,)), ((), ()))
TN_DIMS = (((0,), (0,)), ((), ()))
NN_DIMS = (((1,), (0,)), ((), ()))


def dot(a, b, dims):
    return lax.dot_general(a, b, dims, preferred_element_type=jnp.float32)


def masks(facts_ref, which, rows, lanes):
    ctx = lax.axis_index("ctx")
    key_index = lax.broadcasted_iota(jnp.int32, (2 * rows, 1), 0)
    col_pos = key_index + (ctx - 1) * rows
    row_pos = lax.rem(lax.broadcasted_iota(jnp.int32, (1, lanes), 1), rows) + ctx * rows
    col_doc = jnp.zeros_like(col_pos)
    row_doc = jnp.zeros_like(row_pos)
    for d in range(NDOC - 1):
        end = facts_ref[which * NDOC + d]
        col_doc = col_doc + (col_pos >= end).astype(jnp.int32)
        row_doc = row_doc + (row_pos >= end).astype(jnp.int32)
    seen = (key_index >= rows) | (facts_ref[which * NDOC + NDOC - 1] == 1)
    col_doc = jnp.where(seen & (col_pos >= 0), col_doc, -1)
    back = row_pos - col_pos
    own = (col_doc == row_doc) & (back >= 0)
    query = (col_doc == 0) & (row_doc != 0)
    return own | query, own & (back < rows // 4), own & (back >= rows // 4), query


def as_factor(mask):
    return jnp.where(mask, 1.0, 0.0).astype(jnp.bfloat16)


def pairing(rows, lanes):
    window = rows // 4
    lane = lax.broadcasted_iota(jnp.int32, (lanes, lanes // 2), 0)
    shared = lax.broadcasted_iota(jnp.int32, (lanes, lanes // 2), 1)
    target = lane // (2 * window) * window + lax.rem(lane, window)
    return as_factor(target == shared)


def stacked_heads(block, rows):
    return jnp.concatenate(
        [block[:, h * HEAD_SIZE : (h + 1) * HEAD_SIZE] for h in range(GROUP_RATIO)], axis=0
    )


def spread_heads(value, rows):
    return jnp.concatenate([value[h * rows : (h + 1) * rows] for h in range(GROUP_RATIO)], axis=1)


def folded(value, bound):
    total = value[:bound]
    for b in range(1, value.shape[0] // bound):
        total = total + value[b * bound : (b + 1) * bound]
    return total


def total(own, arrived):
    arrived = jnp.where(lax.axis_index("ctx") == 0, arrived.astype(jnp.float32), 0.0)
    return (own + arrived).astype(jnp.bfloat16)


def scores_body(
    far, slot, first, passed, rows,
    q_ref, g_ref, k_ref, v_ref, first_k_ref, first_v_ref, passed_k_ref, passed_v_ref, bias_ref, *rest
):
    lanes = GROUP_RATIO * rows
    window = rows // 4
    if far:
        factors_ref, pairing_ref, out_hbm, own_ref, leaving_ref, out_ref, shared_ref, sem = rest
        recent_ref, older_ref, far_ref = (factors_ref.at[i] for i in range(3))
        store = pltpu.make_async_copy(out_ref, out_hbm, sem)
    elif len(rest) > 3:
        before_ref, out_ref, own_ref, leaving_ref, grads_ref = rest
        for which, ref in ((0, first_k_ref), (1, first_v_ref)):
            grads_ref[which] = total(before_ref[which], ref[first[which]])
    else:
        out_ref, own_ref, leaving_ref = rest
    sends = lax.axis_index("ctx") == 0

    def middle(scores, dprobs):
        scores = scores * (SCALE * LOG2_E) + bias_ref[slot]
        expd = jnp.exp2(scores - jnp.max(scores, axis=0, keepdims=True))
        inverse = 1.0 / jnp.sum(expd, axis=0, keepdims=True)
        delta = jnp.sum(expd * dprobs, axis=0, keepdims=True) * inverse
        probs = (expd * inverse).astype(jnp.bfloat16)
        return probs, (expd * (inverse * SCALE) * (dprobs - delta)).astype(jnp.bfloat16)

    units = range(KEY_VALUE_HEADS)
    feats = [pl.ds(u * HEAD_SIZE, HEAD_SIZE) for u in units]
    wide = [pl.ds(u * WIDE, WIDE) for u in units]
    q = [stacked_heads(q_ref[slot, :, w], rows) for w in wide]
    g = [stacked_heads(g_ref[slot, :, w], rows) for w in wide]
    k = [jnp.concatenate([first_k_ref[first[0], :, f], k_ref[slot, :, f]], axis=0) for f in feats]
    v = [jnp.concatenate([first_v_ref[first[1], :, f], v_ref[slot, :, f]], axis=0) for f in feats]
    scores = [dot(a, b, NT_DIMS) for a, b in zip(k, q)]
    dprobs = [dot(a, b, NT_DIMS) for a, b in zip(v, g)]
    pairs = [middle(a, b) for a, b in zip(scores, dprobs)]
    for n, u in enumerate(units):
        if not far:
            out_ref[0, u], out_ref[1, u] = pairs[n]
            continue
        span = pl.ds(u * lanes, lanes)
        base = far + far % window
        ahead = [folded(value * far_ref[...], base) for value in pairs[n]]
        if base > far:
            ahead = [value.astype(jnp.float32)[:far] for value in ahead]
        out_ref[: 2 * far, span] = jnp.concatenate(ahead, axis=0).astype(jnp.bfloat16)
        for which, value in enumerate(pairs[n]):
            top = 2 * far + which * window
            out_ref[top : top + window, span] = folded(value * recent_ref[...], window)
            place = (which * KEY_VALUE_HEADS + u) * window
            shared_ref[pl.ds(place, window)] = folded(value * older_ref[...], window)
    if far:
        shared = dot(shared_ref[...], pairing_ref[...], NN_DIMS).astype(jnp.bfloat16)
        for n in range(2 * KEY_VALUE_HEADS):
            span = pl.ds(n * lanes // 2, lanes // 2)
            out_ref[2 * (far + window) :, span] = shared[n * window : (n + 1) * window]
        store.start()
    for which, sides in ((0, q), (1, g)):
        passed_ref = (passed_k_ref, passed_v_ref)[which]
        for n, f in enumerate(feats):
            grad = dot(pairs[n][1 - which], sides[n], NN_DIMS)
            own_ref[which, :, f] = grad[rows:]
            leaving_ref[which, :, f] = jnp.where(
                sends, passed_ref[passed[which], :, f], grad[:rows].astype(jnp.bfloat16)
            )
    if far:
        store.wait()


def scores(far, slot, q, g, k, v, first, passed, bias, *more):
    rows = q.shape[1]
    lanes = GROUP_RATIO * rows
    vmem = pl.BlockSpec(memory_space=pltpu.VMEM)
    anywhere = pl.BlockSpec(memory_space=pl.ANY)
    partial = (2, *k.shape[1:])
    leaving = jax.ShapeDtypeStruct(partial, jnp.bfloat16)
    scratch = []
    if far:
        coded = (2 * far + 3 * rows // 4, KEY_VALUE_HEADS * lanes)
        out_specs = [anywhere, vmem, vmem]
        out_shape = [pltpu.HBM(coded, jnp.bfloat16), jax.ShapeDtypeStruct(partial, jnp.float32), leaving]
        scratch = [
            pltpu.VMEM(coded, jnp.bfloat16),
            pltpu.VMEM((2 * KEY_VALUE_HEADS * rows // 4, lanes), jnp.bfloat16),
            pltpu.SemaphoreType.DMA,
        ]
    else:
        coded = (2, KEY_VALUE_HEADS, 2 * rows, lanes)
        out_specs = [vmem] * (3 + len(more))
        out_shape = [
            jax.ShapeDtypeStruct(coded, jnp.bfloat16),
            jax.ShapeDtypeStruct(partial, jnp.float32),
            leaving,
        ] + [leaving for _ in more]
    return pl.pallas_call(
        functools.partial(
            scores_body, far, slot, (first[0][1], first[1][1]), (passed[0][1], passed[1][1]), rows
        ),
        in_specs=[vmem] * (9 + len(more)),
        out_specs=out_specs,
        out_shape=out_shape,
        scratch_shapes=scratch,
        compiler_params=PARAMS,
        cost_estimate=CHEAP,
    )(q, g, k, v, first[0][0], first[1][0], passed[0][0], passed[1][0], bias, *more)


def prepare_body(
    rows, lengths_in, tiles_in, q_in, g_in, k_in, v_in,
    bias_ref, factors_ref, partner_ref, pairing_ref, q_ref, g_ref, k_ref, v_ref,
    lengths_ref, tiles_ref, facts_ref, scalar_sems, sems,
):
    scalars = ((lengths_in, lengths_ref), (tiles_in, tiles_ref))
    scalars = [pltpu.make_async_copy(a, b, scalar_sems.at[i]) for i, (a, b) in enumerate(scalars)]
    for load in scalars:
        load.start()
    loads = ((q_in, q_ref), (g_in, g_ref), (k_in, k_ref), (v_in, v_ref))
    loads = [pltpu.make_async_copy(a, b, sems.at[i]) for i, (a, b) in enumerate(loads)]
    for load in loads:
        load.start()
    for load in scalars:
        load.wait()
    rank = lax.axis_index("dp")
    ctx = lax.axis_index("ctx")
    partner = jnp.bitwise_xor(rank, lax.axis_size("dp") // 2)
    for which, seq in enumerate((2 * rank, 2 * rank + 1, 2 * partner + 1)):
        end = jnp.int32(0)
        for d in range(NDOC - 1):
            end = end + lengths_ref[d, seq]
            facts_ref[which * NDOC + d] = end
        facts_ref[which * NDOC + NDOC - 1] = tiles_ref[ctx, 0, seq]
    lanes = GROUP_RATIO * rows
    for slot in range(2):
        allowed, *parts = masks(facts_ref, slot, rows, lanes)
        bias_ref[slot] = jnp.where(allowed, 0.0, -1e30)
    for ref, parts in ((factors_ref, parts), (partner_ref, masks(facts_ref, 2, rows, lanes)[1:])):
        for i, part in enumerate(parts):
            ref[i] = as_factor(part)
    pairing_ref[...] = pairing(rows, lanes)
    for load in loads:
        load.wait()


def prepare(lengths, tiles, q, g, k, v):
    rows = q.shape[1]
    lanes = GROUP_RATIO * rows
    vmem = pl.BlockSpec(memory_space=pltpu.VMEM)
    anywhere = pl.BlockSpec(memory_space=pl.ANY)
    return pl.pallas_call(
        functools.partial(prepare_body, rows),
        in_specs=[anywhere] * 6,
        out_specs=[vmem] * 8,
        out_shape=[
            jax.ShapeDtypeStruct((2, 2 * rows, lanes), jnp.float32),
            jax.ShapeDtypeStruct((3, 2 * rows, lanes), jnp.bfloat16),
            jax.ShapeDtypeStruct((3, 2 * rows, lanes), jnp.bfloat16),
            jax.ShapeDtypeStruct((lanes, lanes // 2), jnp.bfloat16),
        ]
        + [jax.ShapeDtypeStruct(x.shape, x.dtype) for x in (q, g, k, v)],
        scratch_shapes=[pltpu.SMEM(x.shape, x.dtype) for x in (lengths, tiles)]
        + [pltpu.SMEM((3 * NDOC,), jnp.int32)]
        + [pltpu.SemaphoreType.DMA((2,)), pltpu.SemaphoreType.DMA((4,))],
        compiler_params=PARAMS,
        cost_estimate=CHEAP,
    )(lengths, tiles, q, g, k, v)


def outputs_body(slot, first, rows, coded_ref, k_ref, v_ref, first_k_ref, first_v_ref, *rest):
    attn_ref, gq_ref = rest[-2:]
    for u in range(KEY_VALUE_HEADS):
        feats = pl.ds(u * HEAD_SIZE, HEAD_SIZE)
        wide = pl.ds(u * GROUP_RATIO * HEAD_SIZE, GROUP_RATIO * HEAD_SIZE)
        v = jnp.concatenate([first_v_ref[first[1], :, feats], v_ref[slot, :, feats]], axis=0)
        attn_ref[:, wide] = spread_heads(dot(coded_ref[0, u], v, TN_DIMS), rows).astype(jnp.bfloat16)
        k = jnp.concatenate([first_k_ref[first[0], :, feats], k_ref[slot, :, feats]], axis=0)
        gq_ref[:, wide] = spread_heads(dot(coded_ref[1, u], k, TN_DIMS), rows).astype(jnp.bfloat16)


def outputs(slot, coded, k, v, first, shape, earlier=()):
    vmem = pl.BlockSpec(memory_space=pltpu.VMEM)
    of_q = pl.BlockSpec((None, *shape[1:]), lambda i: (slot, 0, 0))
    return pl.pallas_call(
        functools.partial(outputs_body, slot, (first[0][1], first[1][1]), shape[1]),
        grid=(1,),
        in_specs=[vmem] * 5 + [pl.BlockSpec(memory_space=pl.ANY) for _ in earlier],
        out_specs=[of_q, of_q],
        out_shape=[pltpu.HBM(shape, jnp.bfloat16)] * 2,
        input_output_aliases={5: 0, 6: 1} if earlier else {},
        compiler_params=PARAMS,
        cost_estimate=CHEAP,
    )(coded, k, v, first[0][0], first[1][0], *earlier)


def rebuild_body(
    far, rows, pack_ref, near_ref, first_ref, zero_ref, factors_ref, pairing_ref, _a, _b, attn_ref, gq_ref, gk_ref, gv_ref
):
    lanes = GROUP_RATIO * rows
    window = rows // 4
    recent, older, query = (factors_ref[i] for i in range(3))
    for which, out_ref in ((0, gk_ref), (1, gv_ref)):
        out_ref[...] = total(zero_ref[which], first_ref[which])
    shared = [
        pack_ref[2 * (far + window) :, pl.ds(n * lanes // 2, lanes // 2)]
        for n in range(2 * KEY_VALUE_HEADS)
    ]
    shared = dot(jnp.concatenate(shared, axis=0), pairing_ref[...], NT_DIMS).astype(jnp.bfloat16)

    def spread(part):
        return jnp.concatenate([part] * (2 * rows // part.shape[0]), axis=0)

    base = far + far % window
    for u in range(KEY_VALUE_HEADS):
        feats = pl.ds(u * HEAD_SIZE, HEAD_SIZE)
        wide = pl.ds(u * WIDE, WIDE)
        span = pl.ds(u * lanes, lanes)
        ahead = pack_ref[: 2 * far, span]
        if base > far:
            ahead = ahead.astype(jnp.float32)
        for which, side_index, out_ref in ((0, 1, attn_ref), (1, 0, gq_ref)):
            near, top = which * KEY_VALUE_HEADS + u, 2 * far + which * window
            side = jnp.concatenate([first_ref[side_index, :, feats], near_ref[side_index, :, feats]], axis=0)
            part = ahead[which * far : (which + 1) * far]
            if base > far:
                empty = jnp.zeros((base - far, lanes), jnp.float32)
                part = jnp.concatenate([part, empty], axis=0).astype(jnp.bfloat16)
            value = spread(part) * query
            value += spread(pack_ref[top : top + window, span]) * recent
            value += spread(shared[near * window : (near + 1) * window]) * older
            out_ref[:, wide] = spread_heads(dot(value, side, TN_DIMS), rows).astype(jnp.bfloat16)


def rebuild(far, pack, kv_near, arrived, own_zero, factors, pairs, attn, gq):
    rows = attn.shape[1]

    def at(array, slot):
        return pl.BlockSpec((None, *array.shape[1:]), lambda i: (slot, 0, 0))

    anywhere = pl.BlockSpec(memory_space=pl.ANY)
    return pl.pallas_call(
        functools.partial(rebuild_body, far, rows),
        grid=(1,),
        in_specs=[pl.BlockSpec(memory_space=pltpu.VMEM)] * 6 + [anywhere, anywhere],
        out_specs=[at(attn, 1), at(gq, 1), at(kv_near, 0), at(kv_near, 0)],
        out_shape=[pltpu.HBM(attn.shape, attn.dtype)] * 2 + [pltpu.HBM(kv_near.shape, kv_near.dtype)] * 2,
        input_output_aliases={6: 0, 7: 1},
        compiler_params=PARAMS,
        cost_estimate=CHEAP,
    )(pack, kv_near, arrived, own_zero, factors, pairs, attn, gq)


def cut_body(
    flags_in, lengths_in, k_ref, v_ref, form_ref, second_ref, flags_ref, lengths_ref, scalar_sems, sems
):
    scalars = ((flags_in, flags_ref), (lengths_in, lengths_ref))
    scalars = [pltpu.make_async_copy(a, b, scalar_sems.at[i]) for i, (a, b) in enumerate(scalars)]
    copies = [
        pltpu.make_async_copy(ref.at[1], second_ref.at[i], sems.at[i])
        for i, ref in enumerate((k_ref, v_ref))
    ]
    for copy in scalars + copies:
        copy.start()
    for copy in scalars:
        copy.wait()
    rank = lax.axis_index("dp")
    partner = jnp.bitwise_xor(rank, lax.axis_size("dp") // 2)
    longest = jnp.maximum(lengths_ref[0, 2 * rank + 1], lengths_ref[0, 2 * partner + 1])
    form_ref[0] = flags_ref[rank] * (1 + lax.div(longest - 1, k_ref.shape[1] // 8))
    for copy in copies:
        copy.wait()


def cut(flags, lengths, k, v):
    smem = pl.BlockSpec(memory_space=pltpu.SMEM)
    vmem = pl.BlockSpec(memory_space=pltpu.VMEM)
    anywhere = pl.BlockSpec(memory_space=pl.ANY)
    whole = jax.ShapeDtypeStruct(k.shape, k.dtype)
    return pl.pallas_call(
        cut_body,
        in_specs=[anywhere] * 4,
        out_specs=[smem, vmem],
        out_shape=[
            jax.ShapeDtypeStruct((1,), jnp.int32),
            whole,
        ],
        scratch_shapes=[pltpu.SMEM(x.shape, x.dtype) for x in (flags, lengths)]
        + [pltpu.SemaphoreType.DMA((2,)), pltpu.SemaphoreType.DMA((2,))],
        cost_estimate=CHEAP,
    )(flags, lengths, k, v)


def finish_body(partner_ref, _a, _b, gk_ref, gv_ref):
    gk_ref[...] = partner_ref[0]
    gv_ref[...] = partner_ref[1]


def finish(grads_partner, gk, gv):
    anywhere = pl.BlockSpec(memory_space=pl.ANY)
    second = pl.BlockSpec((None, *gk.shape[1:]), lambda i: (1, 0, 0))
    return pl.pallas_call(
        finish_body,
        grid=(1,),
        in_specs=[pl.BlockSpec(gk.shape, lambda i: (0, 0, 0)), anywhere, anywhere],
        out_specs=[second, second],
        out_shape=[pltpu.HBM(gk.shape, gk.dtype)] * 2,
        input_output_aliases={1: 0, 2: 1},
        compiler_params=PARAMS,
        cost_estimate=CHEAP,
    )(grads_partner, gk, gv)


def swapped(value):
    return lax.ppermute(value, "ctx", [(0, 1), (1, 0)])


def to_partner(value):
    size = lax.axis_size("dp")
    return lax.ppermute(value, "dp", [(s, s ^ (size // 2)) for s in range(size)])


def stay(q, k, v, g, lengths, tiles, second):
    bias, _, _, _, q, g, k, v = prepare(lengths, tiles, q, g, k, v)
    arrived = swapped(second)
    first = ((arrived, 0), (arrived, 1))
    coded, own, leaving = scores(0, 1, q, g, k, v, first, ((k, 0), (v, 0)), bias)
    arrived = swapped(leaving)
    done = outputs(1, coded, k, v, first, q.shape)
    first = ((arrived, 0), (arrived, 1))
    coded, own, leaving, grads = scores(0, 0, q, g, k, v, first, ((k, 0), (v, 0)), bias, own)
    arrived = swapped(leaving)
    done = outputs(0, coded, k, v, first, q.shape, done)
    zero = total(own, arrived)
    return *done, jnp.stack([zero[0], grads[0]]), jnp.stack([zero[1], grads[1]])


def trade(far, q, k, v, g, lengths, tiles, second):
    bias, factors, partner_factors, pairs, q, g, k, v = prepare(lengths, tiles, q, g, k, v)
    arrived = swapped(second)
    kv_partner = to_partner(second)
    pack, own, leaving = scores(
        far, 1, q, g, k, v, ((arrived, 0), (arrived, 1)), ((k, 0), (v, 0)), bias, factors, pairs
    )
    arrived = swapped(leaving)
    pack_partner = to_partner(pack)
    first = ((arrived, 0), (arrived, 1))
    coded, own, leaving, grads = scores(
        0, 0, q, g, k, v, first, ((kv_partner, 0), (kv_partner, 1)), bias, own
    )
    arrived = swapped(leaving)
    grads_partner = to_partner(grads)
    attn, gq = outputs(0, coded, k, v, first, q.shape)
    attn, gq, gk, gv = rebuild(
        far, pack_partner, kv_partner, arrived, own, partner_factors, pairs, attn, gq
    )
    return attn, gq, *finish(grads_partner, gk, gv)


def two_rank_shards(query_proj, key_proj, value_proj, grad_attn, doc_lengths, mask_tiles, pair_flags):
    rows = query_proj.shape[1]
    lengths, tiles = doc_lengths.T, mask_tiles.transpose(1, 2, 0)
    form, second = cut(pair_flags, lengths, key_proj, value_proj)
    forms = [stay] + [functools.partial(trade, n * (rows // 8)) for n in range(1, 5)]
    return lax.switch(form[0], forms, query_proj, key_proj, value_proj, grad_attn, lengths, tiles, second)


def from_partner(value, axis, distance):
    mask = 2**distance
    pairs = [(source, source ^ mask) for source in range(lax.axis_size(axis))]
    return lax.ppermute(value, axis, pairs)


def sequence_core(
    query_rows, sequence_keys, sequence_values, sequence_gradients, lengths, tile_table, row_start
):
    rows = query_rows.shape[0]
    length_total = sequence_keys.shape[0]
    groups = sequence_keys.shape[1] // HEAD_SIZE
    group_ratio = QUERY_HEADS // KEY_VALUE_HEADS
    scale = HEAD_SIZE ** (-0.5)
    row_pos = row_start + jnp.arange(rows, dtype=jnp.int32)
    col_pos = jnp.arange(length_total, dtype=jnp.int32)
    ends = jnp.cumsum(lengths)[:-1]
    row_doc = jnp.sum((row_pos[:, None] >= ends[None, :]).astype(jnp.int32), axis=1)
    col_doc = jnp.sum((col_pos[:, None] >= ends[None, :]).astype(jnp.int32), axis=1)
    tile_count = tile_table.shape[0]
    tile_len = length_total // tile_count
    tile_ids = jnp.arange(tile_count, dtype=jnp.int32)
    row_pick = ((row_pos // tile_len)[:, None] == tile_ids[None, :]).astype(jnp.float32)
    col_pick = ((col_pos // tile_len)[:, None] == tile_ids[None, :]).astype(jnp.float32)
    tile_map = jnp.dot(jnp.dot(row_pick, tile_table.astype(jnp.float32)), col_pick.T) > 0.5
    allowed = (
        (col_pos[None, :] <= row_pos[:, None])
        & ((col_doc[None, :] == row_doc[:, None]) | (col_doc[None, :] == 0))
        & tile_map
    )
    heads_of_queries = query_rows.reshape(rows, groups, group_ratio, HEAD_SIZE)
    heads_of_keys = sequence_keys.reshape(length_total, groups, HEAD_SIZE)
    heads_of_values = sequence_values.reshape(length_total, groups, HEAD_SIZE)
    head_gradients = sequence_gradients.reshape(rows, groups, group_ratio, HEAD_SIZE)
    scores = (
        jnp.einsum(
            "igrd,jgd->grij", heads_of_queries, heads_of_keys, preferred_element_type=jnp.float32
        )
        * scale
    )
    scores = jnp.where(allowed, scores, -1e30)
    peak = jnp.max(scores, axis=-1, keepdims=True)
    expd = jnp.where(allowed, jnp.exp(scores - peak), 0.0)
    probs = expd / jnp.sum(expd, axis=-1, keepdims=True)
    probs_b = probs.astype(jnp.bfloat16)
    attn = jnp.einsum(
        "grij,jgd->igrd", probs_b, heads_of_values, preferred_element_type=jnp.float32
    ).astype(jnp.bfloat16)
    delta = jnp.transpose(
        jnp.sum(head_gradients.astype(jnp.float32) * attn.astype(jnp.float32), axis=-1), (1, 2, 0)
    )
    value_gradient = jnp.einsum(
        "grij,igrd->jgd", probs_b, head_gradients, preferred_element_type=jnp.float32
    )
    dprobs = jnp.einsum(
        "igrd,jgd->grij", head_gradients, heads_of_values, preferred_element_type=jnp.float32
    )
    dscores = (probs * (dprobs - delta[..., None]) * scale).astype(jnp.bfloat16)
    grad_q = jnp.einsum(
        "grij,jgd->igrd", dscores, heads_of_keys, preferred_element_type=jnp.float32
    )
    key_gradient = jnp.einsum(
        "grij,igrd->jgd", dscores, heads_of_queries, preferred_element_type=jnp.float32
    )
    return (
        attn.reshape(rows, -1),
        grad_q.astype(jnp.bfloat16).reshape(rows, -1),
        key_gradient.reshape(length_total, -1),
        value_gradient.reshape(length_total, -1),
    )


def attend(query_rows, keys_in, values_in, grads_in, lengths_all, tiles_all, first_id, second_id):
    seq_ids = jnp.stack([first_id, second_id])
    lengths_pair = jnp.take(lengths_all, seq_ids, axis=0)
    tiles_pair = jnp.take(tiles_all, seq_ids, axis=0)
    ctx_rank = lax.axis_index("ctx")
    seq_dev = query_rows.shape[1]
    keys_all, values_all = (
        lax.all_gather(keys_in, "ctx", axis=1, tiled=True),
        lax.all_gather(values_in, "ctx", axis=1, tiled=True),
    )
    pieces = [
        sequence_core(
            query_rows[seq_slot],
            keys_all[seq_slot],
            values_all[seq_slot],
            grads_in[seq_slot],
            lengths_pair[seq_slot],
            tiles_pair[seq_slot],
            ctx_rank * seq_dev,
        )
        for seq_slot in range(2)
    ]
    attn = jnp.stack([pieces[0][0], pieces[1][0]])
    grad_q = jnp.stack([pieces[0][1], pieces[1][1]])
    key_terms = jnp.stack([pieces[0][2], pieces[1][2]])
    value_terms = jnp.stack([pieces[0][3], pieces[1][3]])
    key_sums, value_sums = (
        lax.psum_scatter(key_terms, "ctx", scatter_dimension=1, tiled=True),
        lax.psum_scatter(value_terms, "ctx", scatter_dimension=1, tiled=True),
    )
    return (attn, grad_q, key_sums.astype(jnp.bfloat16), value_sums.astype(jnp.bfloat16))


def take_second(mine, arrived, swapped):
    return jnp.stack([mine[0], jnp.where(swapped, arrived, mine[1])])


def shards(query_proj, key_proj, value_proj, grad_attn, doc_lengths, mask_tiles, pair_flags):
    dp_size = lax.axis_size("dp")
    dp_rank = lax.axis_index("dp")
    far_bit = dp_size.bit_length() - 2
    partner = jnp.bitwise_xor(dp_rank, dp_size // 2)
    pair_flag = lax.dynamic_index_in_dim(pair_flags, dp_rank, 0, keepdims=False)
    swapped = pair_flag == 1
    first_id = 2 * dp_rank
    second_id = jnp.where(swapped, 2 * partner + 1, 2 * dp_rank + 1)
    arrived = from_partner((query_proj[1], key_proj[1], value_proj[1], grad_attn[1]), "dp", far_bit)
    query_now = take_second(query_proj, arrived[0], swapped)
    key_now = take_second(key_proj, arrived[1], swapped)
    value_now = take_second(value_proj, arrived[2], swapped)
    grad_now = take_second(grad_attn, arrived[3], swapped)
    return attend(
        query_now, key_now, value_now, grad_now, doc_lengths, mask_tiles, first_id, second_id
    )


def solution(mesh):
    in_specs = (
        P("dp", "ctx", None),
        P("dp", "ctx", None),
        P("dp", "ctx", None),
        P("dp", "ctx", None),
        P(),
        P(),
        P(),
    )
    out_specs = (
        P("dp", "ctx", None),
        P("dp", "ctx", None),
        P("dp", "ctx", None),
        P("dp", "ctx", None),
    )
    form = two_rank_shards if mesh.shape["ctx"] == 2 else shards
    return jax.shard_map(form, mesh=mesh, in_specs=in_specs, out_specs=out_specs, check_vma=False)
```

```python
import functools

import jax
import jax.numpy as jnp
from jax import lax
from jax.experimental import pallas as pl
from jax.experimental.pallas import tpu as pltpu
from jax.sharding import PartitionSpec as P

QUERY_HEADS = 32
KEY_VALUE_HEADS = 8
HEAD_SIZE = 128
GROUP_RATIO = QUERY_HEADS // KEY_VALUE_HEADS
SCALE = HEAD_SIZE ** (-0.5)
LOG2_E = 1.4426950408889634
WIDE = GROUP_RATIO * HEAD_SIZE
NDOC = 8
PARAMS = pltpu.CompilerParams(vmem_limit_bytes=32 * 2**20)
CHEAP = pl.CostEstimate(flops=1, bytes_accessed=1, transcendentals=0)
NT_DIMS = (((1,), (1,)), ((), ()))
TN_DIMS = (((0,), (0,)), ((), ()))
NN_DIMS = (((1,), (0,)), ((), ()))


def dot(a, b, dims):
    return lax.dot_general(a, b, dims, preferred_element_type=jnp.float32)


def masks(facts_ref, which, rows, lanes):
    ctx = lax.axis_index("ctx")
    key_index = lax.broadcasted_iota(jnp.int32, (2 * rows, 1), 0)
    col_pos = key_index + (ctx - 1) * rows
    row_pos = lax.rem(lax.broadcasted_iota(jnp.int32, (1, lanes), 1), rows) + ctx * rows
    col_doc = jnp.zeros_like(col_pos)
    row_doc = jnp.zeros_like(row_pos)
    for d in range(NDOC - 1):
        end = facts_ref[which * NDOC + d]
        col_doc = col_doc + (col_pos >= end).astype(jnp.int32)
        row_doc = row_doc + (row_pos >= end).astype(jnp.int32)
    seen = (key_index >= rows) | (facts_ref[which * NDOC + NDOC - 1] == 1)
    col_doc = jnp.where(seen & (col_pos >= 0), col_doc, -1)
    back = row_pos - col_pos
    own = (col_doc == row_doc) & (back >= 0)
    query = (col_doc == 0) & (row_doc != 0)
    return own | query, own & (back < rows // 4), own & (back >= rows // 4), query


def as_factor(mask):
    return jnp.where(mask, 1.0, 0.0).astype(jnp.bfloat16)


def pairing(rows, lanes):
    window = rows // 4
    lane = lax.broadcasted_iota(jnp.int32, (lanes, lanes // 2), 0)
    shared = lax.broadcasted_iota(jnp.int32, (lanes, lanes // 2), 1)
    target = lane // (2 * window) * window + lax.rem(lane, window)
    return as_factor(target == shared)


def stacked_heads(block, rows):
    return jnp.concatenate(
        [block[:, h * HEAD_SIZE : (h + 1) * HEAD_SIZE] for h in range(GROUP_RATIO)], axis=0
    )


def spread_heads(value, rows):
    return jnp.concatenate([value[h * rows : (h + 1) * rows] for h in range(GROUP_RATIO)], axis=1)


def folded(value, bound):
    total = value[:bound]
    for b in range(1, value.shape[0] // bound):
        total = total + value[b * bound : (b + 1) * bound]
    return total


def total(own, arrived):
    arrived = jnp.where(lax.axis_index("ctx") == 0, arrived.astype(jnp.float32), 0.0)
    return (own + arrived).astype(jnp.bfloat16)


def scores_body(
    far, slot, first, passed, rows,
    q_ref, g_ref, k_ref, v_ref, first_k_ref, first_v_ref, passed_k_ref, passed_v_ref, bias_ref, *rest
):
    lanes = GROUP_RATIO * rows
    window = rows // 4
    if far:
        factors_ref, pairing_ref, out_hbm, own_ref, leaving_ref, out_ref, shared_ref, sem = rest
        recent_ref, older_ref, far_ref = (factors_ref.at[i] for i in range(3))
        store = pltpu.make_async_copy(out_ref, out_hbm, sem)
    elif len(rest) > 3:
        before_ref, out_ref, own_ref, leaving_ref, grads_ref = rest
        for which, ref in ((0, first_k_ref), (1, first_v_ref)):
            grads_ref[which] = total(before_ref[which], ref[first[which]])
    else:
        out_ref, own_ref, leaving_ref = rest
    sends = lax.axis_index("ctx") == 0

    def middle(scores, dprobs):
        scores = scores * (SCALE * LOG2_E) + bias_ref[slot]
        expd = jnp.exp2(scores - jnp.max(scores, axis=0, keepdims=True))
        inverse = 1.0 / jnp.sum(expd, axis=0, keepdims=True)
        delta = jnp.sum(expd * dprobs, axis=0, keepdims=True) * inverse
        probs = (expd * inverse).astype(jnp.bfloat16)
        return probs, (expd * (inverse * SCALE) * (dprobs - delta)).astype(jnp.bfloat16)

    units = range(KEY_VALUE_HEADS)
    feats = [pl.ds(u * HEAD_SIZE, HEAD_SIZE) for u in units]
    wide = [pl.ds(u * WIDE, WIDE) for u in units]
    q = [stacked_heads(q_ref[slot, :, w], rows) for w in wide]
    g = [stacked_heads(g_ref[slot, :, w], rows) for w in wide]
    k = [jnp.concatenate([first_k_ref[first[0], :, f], k_ref[slot, :, f]], axis=0) for f in feats]
    v = [jnp.concatenate([first_v_ref[first[1], :, f], v_ref[slot, :, f]], axis=0) for f in feats]
    scores = [dot(a, b, NT_DIMS) for a, b in zip(k, q)]
    dprobs = [dot(a, b, NT_DIMS) for a, b in zip(v, g)]
    pairs = [middle(a, b) for a, b in zip(scores, dprobs)]
    for n, u in enumerate(units):
        if not far:
            out_ref[0, u], out_ref[1, u] = pairs[n]
            continue
        span = pl.ds(u * lanes, lanes)
        base = far + far % window
        ahead = [folded(value * far_ref[...], base) for value in pairs[n]]
        if base > far:
            ahead = [value.astype(jnp.float32)[:far] for value in ahead]
        out_ref[: 2 * far, span] = jnp.concatenate(ahead, axis=0).astype(jnp.bfloat16)
        for which, value in enumerate(pairs[n]):
            top = 2 * far + which * window
            out_ref[top : top + window, span] = folded(value * recent_ref[...], window)
            place = (which * KEY_VALUE_HEADS + u) * window
            shared_ref[pl.ds(place, window)] = folded(value * older_ref[...], window)
    if far:
        shared = dot(shared_ref[...], pairing_ref[...], NN_DIMS).astype(jnp.bfloat16)
        for n in range(2 * KEY_VALUE_HEADS):
            span = pl.ds(n * lanes // 2, lanes // 2)
            out_ref[2 * (far + window) :, span] = shared[n * window : (n + 1) * window]
        store.start()
    for which, sides in ((0, q), (1, g)):
        passed_ref = (passed_k_ref, passed_v_ref)[which]
        for n, f in enumerate(feats):
            grad = dot(pairs[n][1 - which], sides[n], NN_DIMS)
            own_ref[which, :, f] = grad[rows:]
            leaving_ref[which, :, f] = jnp.where(
                sends, passed_ref[passed[which], :, f], grad[:rows].astype(jnp.bfloat16)
            )
    if far:
        store.wait()


def scores(far, slot, q, g, k, v, first, passed, bias, *more):
    rows = q.shape[1]
    lanes = GROUP_RATIO * rows
    vmem = pl.BlockSpec(memory_space=pltpu.VMEM)
    anywhere = pl.BlockSpec(memory_space=pl.ANY)
    partial = (2, *k.shape[1:])
    leaving = jax.ShapeDtypeStruct(partial, jnp.bfloat16)
    scratch = []
    if far:
        coded = (2 * far + 3 * rows // 4, KEY_VALUE_HEADS * lanes)
        out_specs = [anywhere, vmem, vmem]
        out_shape = [pltpu.HBM(coded, jnp.bfloat16), jax.ShapeDtypeStruct(partial, jnp.float32), leaving]
        scratch = [
            pltpu.VMEM(coded, jnp.bfloat16),
            pltpu.VMEM((2 * KEY_VALUE_HEADS * rows // 4, lanes), jnp.bfloat16),
            pltpu.SemaphoreType.DMA,
        ]
    else:
        coded = (2, KEY_VALUE_HEADS, 2 * rows, lanes)
        out_specs = [vmem] * (3 + len(more))
        out_shape = [
            jax.ShapeDtypeStruct(coded, jnp.bfloat16),
            jax.ShapeDtypeStruct(partial, jnp.float32),
            leaving,
        ] + [leaving for _ in more]
    return pl.pallas_call(
        functools.partial(
            scores_body, far, slot, (first[0][1], first[1][1]), (passed[0][1], passed[1][1]), rows
        ),
        in_specs=[vmem] * (9 + len(more)),
        out_specs=out_specs,
        out_shape=out_shape,
        scratch_shapes=scratch,
        compiler_params=PARAMS,
        cost_estimate=CHEAP,
    )(q, g, k, v, first[0][0], first[1][0], passed[0][0], passed[1][0], bias, *more)


def prepare_body(
    rows, lengths_in, tiles_in, q_in, g_in, k_in, v_in,
    bias_ref, factors_ref, partner_ref, pairing_ref, q_ref, g_ref, k_ref, v_ref,
    lengths_ref, tiles_ref, facts_ref, scalar_sems, sems,
):
    scalars = ((lengths_in, lengths_ref), (tiles_in, tiles_ref))
    scalars = [pltpu.make_async_copy(a, b, scalar_sems.at[i]) for i, (a, b) in enumerate(scalars)]
    for load in scalars:
        load.start()
    loads = ((q_in, q_ref), (g_in, g_ref), (k_in, k_ref), (v_in, v_ref))
    loads = [pltpu.make_async_copy(a, b, sems.at[i]) for i, (a, b) in enumerate(loads)]
    for load in loads:
        load.start()
    for load in scalars:
        load.wait()
    rank = lax.axis_index("dp")
    ctx = lax.axis_index("ctx")
    partner = jnp.bitwise_xor(rank, lax.axis_size("dp") // 2)
    for which, seq in enumerate((2 * rank, 2 * rank + 1, 2 * partner + 1)):
        end = jnp.int32(0)
        for d in range(NDOC - 1):
            end = end + lengths_ref[d, seq]
            facts_ref[which * NDOC + d] = end
        facts_ref[which * NDOC + NDOC - 1] = tiles_ref[ctx, 0, seq]
    lanes = GROUP_RATIO * rows
    for slot in range(2):
        allowed, *parts = masks(facts_ref, slot, rows, lanes)
        bias_ref[slot] = jnp.where(allowed, 0.0, -1e30)
    for ref, parts in ((factors_ref, parts), (partner_ref, masks(facts_ref, 2, rows, lanes)[1:])):
        for i, part in enumerate(parts):
            ref[i] = as_factor(part)
    pairing_ref[...] = pairing(rows, lanes)
    for load in loads:
        load.wait()


def prepare(lengths, tiles, q, g, k, v):
    rows = q.shape[1]
    lanes = GROUP_RATIO * rows
    vmem = pl.BlockSpec(memory_space=pltpu.VMEM)
    anywhere = pl.BlockSpec(memory_space=pl.ANY)
    return pl.pallas_call(
        functools.partial(prepare_body, rows),
        in_specs=[anywhere] * 6,
        out_specs=[vmem] * 8,
        out_shape=[
            jax.ShapeDtypeStruct((2, 2 * rows, lanes), jnp.float32),
            jax.ShapeDtypeStruct((3, 2 * rows, lanes), jnp.bfloat16),
            jax.ShapeDtypeStruct((3, 2 * rows, lanes), jnp.bfloat16),
            jax.ShapeDtypeStruct((lanes, lanes // 2), jnp.bfloat16),
        ]
        + [jax.ShapeDtypeStruct(x.shape, x.dtype) for x in (q, g, k, v)],
        scratch_shapes=[pltpu.SMEM(x.shape, x.dtype) for x in (lengths, tiles)]
        + [pltpu.SMEM((3 * NDOC,), jnp.int32)]
        + [pltpu.SemaphoreType.DMA((2,)), pltpu.SemaphoreType.DMA((4,))],
        compiler_params=PARAMS,
        cost_estimate=CHEAP,
    )(lengths, tiles, q, g, k, v)


def outputs_body(slot, first, rows, coded_ref, k_ref, v_ref, first_k_ref, first_v_ref, *rest):
    attn_ref, gq_ref = rest[-2:]
    for u in range(KEY_VALUE_HEADS):
        feats = pl.ds(u * HEAD_SIZE, HEAD_SIZE)
        wide = pl.ds(u * GROUP_RATIO * HEAD_SIZE, GROUP_RATIO * HEAD_SIZE)
        v = jnp.concatenate([first_v_ref[first[1], :, feats], v_ref[slot, :, feats]], axis=0)
        attn_ref[:, wide] = spread_heads(dot(coded_ref[0, u], v, TN_DIMS), rows).astype(jnp.bfloat16)
        k = jnp.concatenate([first_k_ref[first[0], :, feats], k_ref[slot, :, feats]], axis=0)
        gq_ref[:, wide] = spread_heads(dot(coded_ref[1, u], k, TN_DIMS), rows).astype(jnp.bfloat16)


def outputs(slot, coded, k, v, first, shape, earlier=()):
    vmem = pl.BlockSpec(memory_space=pltpu.VMEM)
    of_q = pl.BlockSpec((None, *shape[1:]), lambda i: (slot, 0, 0))
    return pl.pallas_call(
        functools.partial(outputs_body, slot, (first[0][1], first[1][1]), shape[1]),
        grid=(1,),
        in_specs=[vmem] * 5 + [pl.BlockSpec(memory_space=pl.ANY) for _ in earlier],
        out_specs=[of_q, of_q],
        out_shape=[pltpu.HBM(shape, jnp.bfloat16)] * 2,
        input_output_aliases={5: 0, 6: 1} if earlier else {},
        compiler_params=PARAMS,
        cost_estimate=CHEAP,
    )(coded, k, v, first[0][0], first[1][0], *earlier)


def rebuild_body(
    far, rows, pack_ref, near_ref, first_ref, zero_ref, factors_ref, pairing_ref, _a, _b, attn_ref, gq_ref, gk_ref, gv_ref
):
    lanes = GROUP_RATIO * rows
    window = rows // 4
    recent, older, query = (factors_ref[i] for i in range(3))
    for which, out_ref in ((0, gk_ref), (1, gv_ref)):
        out_ref[...] = total(zero_ref[which], first_ref[which])
    shared = [
        pack_ref[2 * (far + window) :, pl.ds(n * lanes // 2, lanes // 2)]
        for n in range(2 * KEY_VALUE_HEADS)
    ]
    shared = dot(jnp.concatenate(shared, axis=0), pairing_ref[...], NT_DIMS).astype(jnp.bfloat16)

    def spread(part):
        return jnp.concatenate([part] * (2 * rows // part.shape[0]), axis=0)

    base = far + far % window
    for u in range(KEY_VALUE_HEADS):
        feats = pl.ds(u * HEAD_SIZE, HEAD_SIZE)
        wide = pl.ds(u * WIDE, WIDE)
        span = pl.ds(u * lanes, lanes)
        ahead = pack_ref[: 2 * far, span]
        if base > far:
            ahead = ahead.astype(jnp.float32)
        for which, side_index, out_ref in ((0, 1, attn_ref), (1, 0, gq_ref)):
            near, top = which * KEY_VALUE_HEADS + u, 2 * far + which * window
            side = jnp.concatenate([first_ref[side_index, :, feats], near_ref[side_index, :, feats]], axis=0)
            part = ahead[which * far : (which + 1) * far]
            if base > far:
                empty = jnp.zeros((base - far, lanes), jnp.float32)
                part = jnp.concatenate([part, empty], axis=0).astype(jnp.bfloat16)
            value = spread(part) * query
            value += spread(pack_ref[top : top + window, span]) * recent
            value += spread(shared[near * window : (near + 1) * window]) * older
            out_ref[:, wide] = spread_heads(dot(value, side, TN_DIMS), rows).astype(jnp.bfloat16)


def rebuild(far, pack, kv_near, arrived, own_zero, factors, pairs, attn, gq):
    rows = attn.shape[1]

    def at(array, slot):
        return pl.BlockSpec((None, *array.shape[1:]), lambda i: (slot, 0, 0))

    anywhere = pl.BlockSpec(memory_space=pl.ANY)
    return pl.pallas_call(
        functools.partial(rebuild_body, far, rows),
        grid=(1,),
        in_specs=[pl.BlockSpec(memory_space=pltpu.VMEM)] * 6 + [anywhere, anywhere],
        out_specs=[at(attn, 1), at(gq, 1), at(kv_near, 0), at(kv_near, 0)],
        out_shape=[pltpu.HBM(attn.shape, attn.dtype)] * 2 + [pltpu.HBM(kv_near.shape, kv_near.dtype)] * 2,
        input_output_aliases={6: 0, 7: 1},
        compiler_params=PARAMS,
        cost_estimate=CHEAP,
    )(pack, kv_near, arrived, own_zero, factors, pairs, attn, gq)


def cut_body(
    flags_in, lengths_in, k_ref, v_ref, form_ref, second_ref, flags_ref, lengths_ref, scalar_sems, sems
):
    scalars = ((flags_in, flags_ref), (lengths_in, lengths_ref))
    scalars = [pltpu.make_async_copy(a, b, scalar_sems.at[i]) for i, (a, b) in enumerate(scalars)]
    copies = [
        pltpu.make_async_copy(ref.at[1], second_ref.at[i], sems.at[i])
        for i, ref in enumerate((k_ref, v_ref))
    ]
    for copy in scalars + copies:
        copy.start()
    for copy in scalars:
        copy.wait()
    rank = lax.axis_index("dp")
    partner = jnp.bitwise_xor(rank, lax.axis_size("dp") // 2)
    longest = jnp.maximum(lengths_ref[0, 2 * rank + 1], lengths_ref[0, 2 * partner + 1])
    form_ref[0] = flags_ref[rank] * (1 + lax.div(longest - 1, k_ref.shape[1] // 8))
    for copy in copies:
        copy.wait()


def cut(flags, lengths, k, v):
    smem = pl.BlockSpec(memory_space=pltpu.SMEM)
    vmem = pl.BlockSpec(memory_space=pltpu.VMEM)
    anywhere = pl.BlockSpec(memory_space=pl.ANY)
    whole = jax.ShapeDtypeStruct(k.shape, k.dtype)
    return pl.pallas_call(
        cut_body,
        in_specs=[anywhere] * 4,
        out_specs=[smem, vmem],
        out_shape=[
            jax.ShapeDtypeStruct((1,), jnp.int32),
            whole,
        ],
        scratch_shapes=[pltpu.SMEM(x.shape, x.dtype) for x in (flags, lengths)]
        + [pltpu.SemaphoreType.DMA((2,)), pltpu.SemaphoreType.DMA((2,))],
        cost_estimate=CHEAP,
    )(flags, lengths, k, v)


def finish_body(partner_ref, _a, _b, gk_ref, gv_ref):
    gk_ref[...] = partner_ref[0]
    gv_ref[...] = partner_ref[1]


def finish(grads_partner, gk, gv):
    anywhere = pl.BlockSpec(memory_space=pl.ANY)
    second = pl.BlockSpec((None, *gk.shape[1:]), lambda i: (1, 0, 0))
    return pl.pallas_call(
        finish_body,
        grid=(1,),
        in_specs=[pl.BlockSpec(gk.shape, lambda i: (0, 0, 0)), anywhere, anywhere],
        out_specs=[second, second],
        out_shape=[pltpu.HBM(gk.shape, gk.dtype)] * 2,
        input_output_aliases={1: 0, 2: 1},
        compiler_params=PARAMS,
        cost_estimate=CHEAP,
    )(grads_partner, gk, gv)


def close_body(own_ref, arrived_ref, second_ref, gk_ref, gv_ref):
    for which, ref in ((0, gk_ref), (1, gv_ref)):
        ref[0] = total(own_ref[which], arrived_ref[which])
        ref[1] = second_ref[which]


def close(own, arrived, second):
    vmem = pl.BlockSpec(memory_space=pltpu.VMEM)
    whole = pl.BlockSpec(second.shape, lambda i: (0, 0, 0))
    return pl.pallas_call(
        close_body,
        grid=(1,),
        in_specs=[vmem] * 3,
        out_specs=[whole, whole],
        out_shape=[pltpu.HBM(second.shape, second.dtype)] * 2,
        compiler_params=PARAMS,
        cost_estimate=CHEAP,
    )(own, arrived, second)


def swapped(value):
    return lax.ppermute(value, "ctx", [(0, 1), (1, 0)])


def to_partner(value):
    size = lax.axis_size("dp")
    return lax.ppermute(value, "dp", [(s, s ^ (size // 2)) for s in range(size)])


def stay(q, k, v, g, lengths, tiles, second):
    bias, _, _, _, q, g, k, v = prepare(lengths, tiles, q, g, k, v)
    arrived = swapped(second)
    first = ((arrived, 0), (arrived, 1))
    coded, own, leaving = scores(0, 1, q, g, k, v, first, ((k, 0), (v, 0)), bias)
    arrived = swapped(leaving)
    done = outputs(1, coded, k, v, first, q.shape)
    arrived, *done = lax.optimization_barrier((arrived, *done))
    first = ((arrived, 0), (arrived, 1))
    coded, own, leaving, grads = scores(0, 0, q, g, k, v, first, ((k, 0), (v, 0)), bias, own)
    arrived = swapped(leaving)
    done = outputs(0, coded, k, v, first, q.shape, done)
    return *done, *close(own, arrived, grads)


def trade(far, q, k, v, g, lengths, tiles, second):
    bias, factors, partner_factors, pairs, q, g, k, v = prepare(lengths, tiles, q, g, k, v)
    arrived = swapped(second)
    kv_partner = to_partner(second)
    pack, own, leaving = scores(
        far, 1, q, g, k, v, ((arrived, 0), (arrived, 1)), ((k, 0), (v, 0)), bias, factors, pairs
    )
    arrived = swapped(leaving)
    pack_partner = to_partner(pack)
    first = ((arrived, 0), (arrived, 1))
    coded, own, leaving, grads = scores(
        0, 0, q, g, k, v, first, ((kv_partner, 0), (kv_partner, 1)), bias, own
    )
    arrived = swapped(leaving)
    grads_partner = to_partner(grads)
    attn, gq = outputs(0, coded, k, v, first, q.shape)
    attn, gq, gk, gv = rebuild(
        far, pack_partner, kv_partner, arrived, own, partner_factors, pairs, attn, gq
    )
    return attn, gq, *finish(grads_partner, gk, gv)


def two_rank_shards(query_proj, key_proj, value_proj, grad_attn, doc_lengths, mask_tiles, pair_flags):
    rows = query_proj.shape[1]
    lengths, tiles = doc_lengths.T, mask_tiles.transpose(1, 2, 0)
    form, second = cut(pair_flags, lengths, key_proj, value_proj)
    forms = [stay] + [functools.partial(trade, n * (rows // 8)) for n in range(1, 5)]
    return lax.switch(form[0], forms, query_proj, key_proj, value_proj, grad_attn, lengths, tiles, second)


def from_partner(value, axis, distance):
    mask = 2**distance
    pairs = [(source, source ^ mask) for source in range(lax.axis_size(axis))]
    return lax.ppermute(value, axis, pairs)


def sequence_core(
    query_rows, sequence_keys, sequence_values, sequence_gradients, lengths, tile_table, row_start
):
    rows = query_rows.shape[0]
    length_total = sequence_keys.shape[0]
    groups = sequence_keys.shape[1] // HEAD_SIZE
    group_ratio = QUERY_HEADS // KEY_VALUE_HEADS
    scale = HEAD_SIZE ** (-0.5)
    row_pos = row_start + jnp.arange(rows, dtype=jnp.int32)
    col_pos = jnp.arange(length_total, dtype=jnp.int32)
    ends = jnp.cumsum(lengths)[:-1]
    row_doc = jnp.sum((row_pos[:, None] >= ends[None, :]).astype(jnp.int32), axis=1)
    col_doc = jnp.sum((col_pos[:, None] >= ends[None, :]).astype(jnp.int32), axis=1)
    tile_count = tile_table.shape[0]
    tile_len = length_total // tile_count
    tile_ids = jnp.arange(tile_count, dtype=jnp.int32)
    row_pick = ((row_pos // tile_len)[:, None] == tile_ids[None, :]).astype(jnp.float32)
    col_pick = ((col_pos // tile_len)[:, None] == tile_ids[None, :]).astype(jnp.float32)
    tile_map = jnp.dot(jnp.dot(row_pick, tile_table.astype(jnp.float32)), col_pick.T) > 0.5
    allowed = (
        (col_pos[None, :] <= row_pos[:, None])
        & ((col_doc[None, :] == row_doc[:, None]) | (col_doc[None, :] == 0))
        & tile_map
    )
    heads_of_queries = query_rows.reshape(rows, groups, group_ratio, HEAD_SIZE)
    heads_of_keys = sequence_keys.reshape(length_total, groups, HEAD_SIZE)
    heads_of_values = sequence_values.reshape(length_total, groups, HEAD_SIZE)
    head_gradients = sequence_gradients.reshape(rows, groups, group_ratio, HEAD_SIZE)
    scores = (
        jnp.einsum(
            "igrd,jgd->grij", heads_of_queries, heads_of_keys, preferred_element_type=jnp.float32
        )
        * scale
    )
    scores = jnp.where(allowed, scores, -1e30)
    peak = jnp.max(scores, axis=-1, keepdims=True)
    expd = jnp.where(allowed, jnp.exp(scores - peak), 0.0)
    probs = expd / jnp.sum(expd, axis=-1, keepdims=True)
    probs_b = probs.astype(jnp.bfloat16)
    attn = jnp.einsum(
        "grij,jgd->igrd", probs_b, heads_of_values, preferred_element_type=jnp.float32
    ).astype(jnp.bfloat16)
    delta = jnp.transpose(
        jnp.sum(head_gradients.astype(jnp.float32) * attn.astype(jnp.float32), axis=-1), (1, 2, 0)
    )
    value_gradient = jnp.einsum(
        "grij,igrd->jgd", probs_b, head_gradients, preferred_element_type=jnp.float32
    )
    dprobs = jnp.einsum(
        "igrd,jgd->grij", head_gradients, heads_of_values, preferred_element_type=jnp.float32
    )
    dscores = (probs * (dprobs - delta[..., None]) * scale).astype(jnp.bfloat16)
    grad_q = jnp.einsum(
        "grij,jgd->igrd", dscores, heads_of_keys, preferred_element_type=jnp.float32
    )
    key_gradient = jnp.einsum(
        "grij,igrd->jgd", dscores, heads_of_queries, preferred_element_type=jnp.float32
    )
    return (
        attn.reshape(rows, -1),
        grad_q.astype(jnp.bfloat16).reshape(rows, -1),
        key_gradient.reshape(length_total, -1),
        value_gradient.reshape(length_total, -1),
    )


def attend(query_rows, keys_in, values_in, grads_in, lengths_all, tiles_all, first_id, second_id):
    seq_ids = jnp.stack([first_id, second_id])
    lengths_pair = jnp.take(lengths_all, seq_ids, axis=0)
    tiles_pair = jnp.take(tiles_all, seq_ids, axis=0)
    ctx_rank = lax.axis_index("ctx")
    seq_dev = query_rows.shape[1]
    keys_all, values_all = (
        lax.all_gather(keys_in, "ctx", axis=1, tiled=True),
        lax.all_gather(values_in, "ctx", axis=1, tiled=True),
    )
    pieces = [
        sequence_core(
            query_rows[seq_slot],
            keys_all[seq_slot],
            values_all[seq_slot],
            grads_in[seq_slot],
            lengths_pair[seq_slot],
            tiles_pair[seq_slot],
            ctx_rank * seq_dev,
        )
        for seq_slot in range(2)
    ]
    attn = jnp.stack([pieces[0][0], pieces[1][0]])
    grad_q = jnp.stack([pieces[0][1], pieces[1][1]])
    key_terms = jnp.stack([pieces[0][2], pieces[1][2]])
    value_terms = jnp.stack([pieces[0][3], pieces[1][3]])
    key_sums, value_sums = (
        lax.psum_scatter(key_terms, "ctx", scatter_dimension=1, tiled=True),
        lax.psum_scatter(value_terms, "ctx", scatter_dimension=1, tiled=True),
    )
    return (attn, grad_q, key_sums.astype(jnp.bfloat16), value_sums.astype(jnp.bfloat16))


def take_second(mine, arrived, swapped):
    return jnp.stack([mine[0], jnp.where(swapped, arrived, mine[1])])


def shards(query_proj, key_proj, value_proj, grad_attn, doc_lengths, mask_tiles, pair_flags):
    dp_size = lax.axis_size("dp")
    dp_rank = lax.axis_index("dp")
    far_bit = dp_size.bit_length() - 2
    partner = jnp.bitwise_xor(dp_rank, dp_size // 2)
    pair_flag = lax.dynamic_index_in_dim(pair_flags, dp_rank, 0, keepdims=False)
    swapped = pair_flag == 1
    first_id = 2 * dp_rank
    second_id = jnp.where(swapped, 2 * partner + 1, 2 * dp_rank + 1)
    arrived = from_partner((query_proj[1], key_proj[1], value_proj[1], grad_attn[1]), "dp", far_bit)
    query_now = take_second(query_proj, arrived[0], swapped)
    key_now = take_second(key_proj, arrived[1], swapped)
    value_now = take_second(value_proj, arrived[2], swapped)
    grad_now = take_second(grad_attn, arrived[3], swapped)
    return attend(
        query_now, key_now, value_now, grad_now, doc_lengths, mask_tiles, first_id, second_id
    )


def solution(mesh):
    in_specs = (
        P("dp", "ctx", None),
        P("dp", "ctx", None),
        P("dp", "ctx", None),
        P("dp", "ctx", None),
        P(),
        P(),
        P(),
    )
    out_specs = (
        P("dp", "ctx", None),
        P("dp", "ctx", None),
        P("dp", "ctx", None),
        P("dp", "ctx", None),
    )
    form = two_rank_shards if mesh.shape["ctx"] == 2 else shards
    return jax.shard_map(form, mesh=mesh, in_specs=in_specs, out_specs=out_specs, check_vma=False)
```
